512 devices in a mesh: space: 32 (over y_hi, z), rep: 16 (over y_lo, x, core).
Axes of the slice: x: 4, y: 4 (y_hi: 2, y_lo: 2; y = y_hi * 2 + y_lo), z: 16, core: 2. Of those that a mesh axis runs over, the one named last changes fastest.
Arguments:
- volumes: bfloat16 [16, 32, 8, 4, 16, 256], P('rep', 'space'), may hold values from -6 to 6
- grad_parts: bfloat16 [16, 2, 6912, 256], P('rep', None, 'space'), may hold values from -6 to 6
- master_weights: float32 [2, 6912, 256], P(None, 'space'), may hold values from -0.078125 to 0.078125
- moment_first: float32 [16, 2, 6912, 256], P('rep', None, 'space'), may hold values from -12 to 12
- moment_second: float32 [16, 2, 6912, 256], P('rep', None, 'space'), may hold values from 1 to 30
- owner: int32 [2, 32], replicated, may hold values from 0 to 15
Outputs:
- features: bfloat16 [16, 32, 8, 4, 16, 256], P('rep', 'space')
- new_weights: float32 [2, 1769472], P(None, ('space', 'rep'))
- moment_first_out: float32 [16, 2, 6912, 256], P('rep', None, 'space')
- moment_second_out: float32 [16, 2, 6912, 256], P('rep', None, 'space')
The draws below stay inside these ranges and needn't reach their ends.
Inputs may be any that keep to these rules, and one draw needn't show every extreme that they name: owner[f, p] is the replica whose state slot holds the optimizer state of panel p of filter f, rows p * 216 to (p + 1) * 216 - 1; replicas may own unequal numbers of panels.
All inputs are finite; a program needn't handle non-finite values.
Results may differ from the reference program's by a relative error of at most 0.0095.
Values may be sent and summed in bfloat16 or wider, within the bound.
A program may use at most 64 MiB of HBM per device.

```python
import math
import jax
import jax.numpy as jnp
import numpy as np
from jax import lax

C = 256
TAPS = 27
FILTERS = 2
PANELS = 32
GY = 2
GZ = 2
BX = 8
BY = 4
BZ = 16
PANEL_ROWS = 216
BRICKS = 32
VOLUMES = 16
N_SPACE = 32
N_REP = 16


def set_ends(entries, own_key, least, high):
    index_at = [jax.random.randint(jax.random.fold_in(own_key, axis), (), 0, length) for axis, length in enumerate(entries.shape)]
    widest = entries.shape.index(max(entries.shape))
    next_to = index_at[:widest] + [(index_at[widest] + 1) % entries.shape[widest]] + index_at[widest + 1:]
    return entries.at[tuple(index_at)].set(least).at[tuple(next_to)].set(high)


def steps_of(key, extent, pieces, least, largest):
    factor_of, own = 1.0, jax.random.fold_in(key, 6)
    for position, blocks in pieces:
        heights = jnp.exp(jax.random.uniform(jax.random.fold_in(own, position), (blocks,), jnp.float32, least / len(pieces), largest / len(pieces)))
        factor_of = factor_of * jnp.repeat(heights, extent[position] // blocks).reshape([-1 if axis == position else 1 for axis in range(len(extent))])
    return factor_of


def rank_table(number_of, lean):
    weights = [(1 << 20) // math.isqrt(grade ** lean) + 1 for grade in range(1, number_of + 1)]
    spread = 1 + sum(weights) // (1 << 30)
    return np.cumsum(np.array([max(1, weight // spread) for weight in weights]))


def skewed_ids(stream_key, extent, amount, lean):
    grid = rank_table(amount, lean)
    lot = jax.random.randint(jax.random.fold_in(stream_key, 1), extent, 0, int(grid[amount - 1]))
    grade = jnp.searchsorted(jnp.asarray(grid, jnp.int32), lot, side="right")
    return jax.random.permutation(jax.random.fold_in(stream_key, 2), amount)[grade].astype(jnp.int32)


def normal_values(own_key, shape, spread, limit, split=(), kind=jnp.bfloat16):
    gain = steps_of(own_key, shape, split, -0.22, 0.18) if split else 1.0
    values = jax.random.normal(own_key, shape, jnp.float32) * spread * gain
    return jnp.minimum(jnp.maximum(values, -limit), limit).astype(kind)


def setup_inputs(seed: int = 0) -> dict:
    splits = jax.random.split(jax.random.key(seed), 7)
    volumes = normal_values(splits[0], (VOLUMES, BRICKS, BX, BY, BZ, C), 1.0, 6.0, ((0, 16), (1, 32)))
    grad_parts = normal_values(splits[1], (VOLUMES, FILTERS, TAPS * C, C), 1.0, 6.0, ((0, 16), (2, 32)))
    master_weights = normal_values(splits[2], (FILTERS, TAPS * C, C), (TAPS * C) ** -0.5, 0.078125, ((1, 32),), jnp.float32)
    moment_first = normal_values(splits[3], (VOLUMES, FILTERS, TAPS * C, C), 2.0, 12.0, ((0, 16), (2, 32)), jnp.float32)
    moment_second = jnp.clip(jnp.exp(math.log(30.0) - 3.4011974 * jax.random.uniform(splits[4], (VOLUMES, FILTERS, TAPS * C, C), jnp.float32) ** steps_of(splits[4], (VOLUMES, FILTERS, TAPS * C, C), ((0, 16), (2, 32)), -0.2, 0.2)), 1.0, 30.0)
    owner = set_ends(skewed_ids(splits[5], (FILTERS, PANELS), N_REP, 2), jax.random.fold_in(splits[5], 3), 0, N_REP - 1).astype(jnp.int32)
    return {"volumes": volumes, "grad_parts": grad_parts, "master_weights": master_weights, "moment_first": moment_first, "moment_second": moment_second, "owner": owner}


def conv_layer(field, filter_rows):
    extent_x, extent_y, extent_z, channels = field.shape
    padded = jnp.pad(field, ((1, 1), (1, 1), (1, 1), (0, 0))).astype(jnp.float32)
    taps_filter = filter_rows.astype(jnp.float32)
    summed = jnp.zeros((extent_x * extent_y * extent_z, taps_filter.shape[1]), jnp.float32)
    for shift_x in range(3):
        for shift_y in range(3):
            for shift_z in range(3):
                tap_index = (shift_x * 3 + shift_y) * 3 + shift_z
                window = padded[shift_x:shift_x + extent_x, shift_y:shift_y + extent_y, shift_z:shift_z + extent_z]
                weights_tap = taps_filter[tap_index * channels:(tap_index + 1) * channels]
                summed = summed + jnp.dot(window.reshape(-1, channels), weights_tap, preferred_element_type=jnp.float32)
    return summed.reshape(extent_x, extent_y, extent_z, -1)

def reference(volumes, grad_parts, master_weights, moment_first, moment_second, owner):
    summed_grad = lax.optimization_barrier(jnp.sum(grad_parts.astype(jnp.float32), axis=0))
    first_new = 0.9 * moment_first + 0.1 * summed_grad[None]
    second_new = 0.95 * moment_second + 0.05 * (summed_grad * summed_grad)[None]
    owner_rows = jnp.repeat(owner, PANEL_ROWS, axis=1)
    replicas = lax.broadcasted_iota(jnp.int32, (N_REP, 1, 1, 1), 0)
    owned = replicas == owner_rows[None, :, :, None]
    first_out = jnp.where(owned, first_new, moment_first)
    second_out = jnp.where(owned, second_new, moment_second)
    first_own = lax.optimization_barrier(jnp.sum(jnp.where(owned, first_new, 0.0), axis=0))
    second_own = lax.optimization_barrier(jnp.sum(jnp.where(owned, second_new, 0.0), axis=0))
    corr_one = 1.0 - 0.9 ** 10
    corr_two = 1.0 - 0.95 ** 10
    update = first_own / corr_one / (jnp.sqrt(second_own / corr_two) + 1e-08) + 0.1 * master_weights
    new_master = master_weights - 0.004 * update
    new_weights = new_master.reshape(FILTERS, -1)
    filters = new_master.astype(jnp.bfloat16)
    grid_x = N_SPACE // (GY * GZ)
    whole = volumes.reshape(N_REP, grid_x, GY, GZ, BX, BY, BZ, C)
    whole = whole.transpose(0, 1, 4, 2, 5, 3, 6, 7).reshape(N_REP, grid_x * BX, GY * BY, GZ * BZ, C)

    def layers(field):
        hidden = jax.nn.gelu(conv_layer(field, filters[0]), approximate=True).astype(jnp.bfloat16)
        return jax.nn.gelu(conv_layer(hidden, filters[1]), approximate=True).astype(jnp.bfloat16)
    result = lax.map(layers, whole)
    result = result.reshape(N_REP, grid_x, BX, GY, BY, GZ, BZ, C).transpose(0, 1, 3, 5, 2, 4, 6, 7)
    features = result.reshape(N_REP, N_SPACE, BX, BY, BZ, C)
    return (features, new_weights, first_out, second_out)
```

```python
import jax
import jax.numpy as jnp
from jax import lax
from jax.experimental import pallas as pl
from jax.experimental.pallas import tpu as pltpu
from jax.sharding import PartitionSpec as P

MESH = pl.DeviceIdType.MESH
F32 = jnp.float32
BF16 = jnp.bfloat16
UNITS = 27
ZS = 16
N_A2A, N_HALO, N_Z, N_RING, N_SIB, N_G = 15, 6, 15, 32, 16, 15


def unit_of(row_unit):
    panel, within = divmod(row_unit, UNITS)
    group, place = divmod(within, 7)
    return panel // ZS, panel % ZS, group // 2, group % 2, place


def runs_of(chunk):
    runs = []
    for k in range(96):
        at = unit_of(96 * chunk + k)
        if runs and runs[-1][1][:4] == at[:4] and runs[-1][1][4] + runs[-1][2] == at[4]:
            runs[-1][2] += 1
        else:
            runs.append([k, at, 1])
    return runs


def gelu(v):
    return 0.5 * v * (1.0 + jnp.tanh(0.7978845608028654 * (v + 0.044715 * (v * v * v))))


def body(
    owner, vol, grads, master, mom1, mom2,
    feat, pan, mom1_out, mom2_out,
    stage, got, gsum, gall, filt, raw, edge_out, edge_in, field, acc, hid, wbuf,
    bar_send, bar_recv,
):
    s = lax.axis_index("space")
    r = lax.axis_index("rep")
    yhi, z = s // ZS, lax.rem(s, ZS)
    ylo, x, c = r // 8, lax.rem(r // 2, 4), lax.rem(r, 2)
    y = 2 * yhi + ylo
    bx, by, bz = s // 4, lax.rem(s // 2, 2), lax.rem(s, 2)

    def device(px, py, pz, pc):
        return (py // 2 * ZS + pz, lax.rem(py, 2) * 8 + 2 * px + pc)

    xp, xm = lax.rem(x + 1, 4), lax.rem(x + 3, 4)
    yp, ym = lax.rem(y + 1, 4), lax.rem(y + 3, 4)
    zp, zm = lax.rem(z + 1, ZS), lax.rem(z + ZS - 1, ZS)
    other_y = jnp.where(ylo == 0, ym, yp)
    peers = [(s, lax.rem(r + d, 16)) for d in range(1, 16)]
    z_peers = [device(x, y, zp, c), device(x, y, zm, c), device(x, other_y, z, c)]
    flip = 2 - 4 * by
    halo_peers = []
    for dx, fl in ((-1, 0), (1, 0), (0, 1), (-1, 1), (1, 1)):
        halo_peers.append((dx, fl, (lax.rem(s + fl * flip + 4 * dx + 32, 32), r)))

    barrier = pltpu.get_barrier_semaphore()
    all_peers = peers + z_peers + [p for _, _, p in halo_peers]
    for p in all_peers:
        pl.semaphore_signal(barrier, inc=1, device_id=p, device_id_type=MESH)

    for d in range(16):
        dl, dx, dc = d // 8, d // 2 % 4, d % 2
        first = 7 * (2 * dc + dl) + 2 * dx
        for u in range(2):
            at = min(first + (u if dx < 3 else 0), UNITS - 1)
            stage[d, :, 0, u] = grads[:, at]
            stage[d, :, 1, u] = mom1[:, at].astype(BF16)
            stage[d, :, 2, u] = mom2[:, at].astype(BF16)

    pl.semaphore_wait(barrier, len(all_peers))

    sent = []
    base = [0]

    def take(n):
        base[0] += n
        return base[0] - n

    def send(src, dst, k, dev):
        copy = pltpu.make_async_remote_copy(
            src_ref=src, dst_ref=dst, send_sem=bar_send.at[k], recv_sem=bar_recv.at[k],
            device_id=dev, device_id_type=MESH,
        )
        copy.start()
        sent.append(copy)

    def arrived(dst, k):
        pltpu.make_async_remote_copy(
            src_ref=dst, dst_ref=dst, send_sem=bar_send.at[k], recv_sem=bar_recv.at[k],
            device_id=(s, r), device_id_type=MESH,
        ).wait_recv()

    a2a = take(N_A2A)
    for d in range(1, 16):
        to = lax.rem(r + d, 16)
        send(stage.at[to], got.at[r], a2a + d - 1, (s, to))
    halo = take(N_HALO)
    x_src = {-1: (0, 2), 0: (0, 8), 1: (6, 2)}
    x_dst = {-1: 10, 0: 2, 1: 0}
    for k, (dx, fl, dev) in enumerate(halo_peers):
        sx, nx = x_src[dx]
        sy, dy, ny = (2 * (1 - by), 6 * by, 2) if fl else (0, 2, 4)
        send(
            vol.at[pl.ds(sx, nx), pl.ds(sy, ny)],
            raw.at[pl.ds(x_dst[dx], nx), pl.ds(dy, ny)],
            halo + k, dev,
        )
    got[r] = stage[r]
    raw[2:10, 2:6] = vol[...]

    for d in range(1, 16):
        arrived(got.at[lax.rem(r + 16 - d, 16)], a2a + d - 1)
    first = 7 * (2 * c + ylo) + 2 * x
    corr_one = 1.0 - 0.9**10
    corr_two = 1.0 - 0.95**10
    for f in range(2):
        own = owner[f, s]
        for u in range(2):
            total = got[0, f, 0, u].astype(F32)
            for k in range(1, 16):
                total = total + got[k, f, 0, u].astype(F32)
            m_new = 0.9 * got[own, f, 1, u].astype(F32) + 0.1 * total
            v_new = 0.95 * got[own, f, 2, u].astype(F32) + 0.05 * (total * total)
            w = master[f, jnp.minimum(first + u, UNITS - 1)]
            step = m_new / corr_one / (jnp.sqrt(v_new / corr_two) + 1e-08) + 0.1 * w
            gsum[f, u] = total.astype(BF16)
            filt[f, yhi, z, c, ylo, 2 * x + u] = (w - 0.004 * step).astype(BF16)

    zb = take(N_Z)

    def z_block(pz):
        return filt.at[:, yhi, pz, c, ylo, pl.ds(2 * x, 2)]

    for k in range(8):
        up, down = lax.rem(z + ZS - k, ZS), lax.rem(z + k, ZS)
        if k:
            arrived(z_block(up), zb + 2 * (k - 1))
        send(z_block(up), z_block(up), zb + 2 * k, device(x, y, zp, c))
        if k:
            arrived(z_block(down), zb + 2 * (k - 1) + 1)
        if k < 7:
            send(z_block(down), z_block(down), zb + 2 * k + 1, device(x, y, zm, c))
    arrived(z_block(lax.rem(z + 8, ZS)), zb + 14)

    ring = take(N_RING)
    sib = take(N_SIB)
    sib_dev = device(x, y, z, 1 - c)

    def region(f, half, phase, pos, part, core):
        z0, nz = 8 * half + (4 if part == 1 else 0), 8 if part is None else 4
        zr = pl.ds(z0, nz)
        if half == 0 and phase == 0:
            return filt.at[f, yhi, zr, core, ylo, pl.ds(2 * pos, 2)]
        if half == 0:
            return filt.at[f, pos // 2, zr, core, lax.rem(pos, 2), pl.ds(0, 7)]
        if phase == 0:
            return filt.at[f, pos // 2, zr, core, lax.rem(pos, 2), pl.ds(2 * x, 2)]
        return filt.at[f, :, zr, core, :, pl.ds(2 * pos, 2)]

    def ring_of(f, half, phase):
        k = ring + 4 * (4 * f + 2 * half + phase)
        if half == phase:
            me, plus, minus, opp = x, xp, xm, lax.rem(x + 2, 4)
            to_plus, to_minus = device(xp, y, z, c), device(xm, y, z, c)
        else:
            me, plus, minus, opp = y, yp, ym, lax.rem(y + 2, 4)
            to_plus, to_minus = device(x, yp, z, c), device(x, ym, z, c)

        def reg(pos, part=None, core=c):
            return region(f, half, phase, pos, part, core)

        return k, me, plus, minus, opp, to_plus, to_minus, reg

    def start_one(f, half, phase):
        k, me, plus, minus, opp, to_plus, to_minus, reg = ring_of(f, half, phase)
        send(reg(me), reg(me), k, to_plus)
        send(reg(me), reg(me), k + 1, to_minus)

    def turn(f, half, phase):
        k, me, plus, minus, opp, to_plus, to_minus, reg = ring_of(f, half, phase)
        arrived(reg(minus), k)
        send(reg(minus, 0), reg(minus, 0), k + 2, to_plus)
        arrived(reg(plus), k + 1)
        send(reg(plus, 1), reg(plus, 1), k + 3, to_minus)
        if phase == 1:
            q = sib + 8 * f + 4 * half + 1
            send(reg(minus), reg(minus), q, sib_dev)
            send(reg(plus), reg(plus), q + 1, sib_dev)

    def end(f, half, phase):
        k, me, plus, minus, opp, to_plus, to_minus, reg = ring_of(f, half, phase)
        arrived(reg(opp, 0), k + 2)
        arrived(reg(opp, 1), k + 3)
        if phase == 1:
            q = sib + 8 * f + 4 * half + 3
            send(reg(opp), reg(opp), q, sib_dev)

    def bulk(f, half):
        k, me, plus, minus, opp, to_plus, to_minus, reg = ring_of(f, half, 1)
        start_one(f, half, 1)
        send(reg(me), reg(me), sib + 8 * f + 4 * half, sib_dev)

    def from_sib(f):
        for half in range(2):
            k, me, plus, minus, opp, to_plus, to_minus, reg = ring_of(f, half, 1)
            for n, pos in enumerate((me, minus, plus, opp)):
                arrived(reg(pos, None, 1 - c), sib + 8 * f + 4 * half + n)

    for f in range(2):
        start_one(f, 0, 0)
        start_one(f, 1, 0)
    for f in range(2):
        turn(f, 0, 0)
        turn(f, 1, 0)
        end(f, 0, 0)
        bulk(f, 0)
        end(f, 1, 0)
        bulk(f, 1)

    for k, (dx, fl, dev) in enumerate(halo_peers):
        sx, nx = x_src[dx]
        dy, ny = (6 * (1 - by), 2) if fl else (2, 4)
        dst_x = {-1: 0, 0: 2, 1: 10}[dx]
        pairs = raw.at[pl.ds(dst_x, nx), pl.ds(dy, ny)]
        arrived(pairs, halo + {0: 1, 1: 0, 2: 2, 3: 4, 4: 3}[k])

    def pack(i, carry):
        rows = [raw[i, j].astype(F32) for j in range(8)]
        near = jnp.concatenate([jnp.where(bz == 0, v[15:16], v[0:1]) for v in rows], axis=0)
        far = jnp.concatenate([jnp.where(bz == 0, v[14:15], v[1:2]) for v in rows], axis=0)
        edge_out[i] = jnp.concatenate([near, far], axis=0).astype(BF16)
        return carry

    lax.fori_loop(0, 12, pack, 0)
    z_partner = z + 1 - 2 * bz
    send(edge_out, edge_in, halo + 5, device(x, y, z_partner, c))
    arrived(edge_in, halo + 5)

    def shifts(i, carry):
        edges = edge_in[i].astype(F32)
        x_ok = (i + 8 * bx >= 2) & (i + 8 * bx < 66)
        for j in range(8):
            y_ok = (j + 4 * by >= 2) & (j + 4 * by < 10)
            ok = x_ok & y_ok
            v = jnp.where(ok, raw[i, j].astype(F32), 0.0)
            e0 = jnp.where(ok, edges[j : j + 1], 0.0)
            e1 = jnp.where(ok, edges[8 + j : 9 + j], 0.0)
            none = jnp.zeros((1, 256), F32)
            rest = jnp.zeros((7, 256), F32)
            low = bz == 0
            field[i, j, :, 0:256] = jnp.concatenate(
                [jnp.where(low, none, e0), v[0:15], jnp.where(low, v[15:16], e1), rest], axis=0
            ).astype(BF16)
            field[i, j, :, 256:512] = jnp.concatenate([v, e0, rest], axis=0).astype(BF16)
            field[i, j, :, 512:768] = jnp.concatenate(
                [v[1:16], jnp.where(low, e0, none), jnp.where(low, e1, v[0:1]), rest], axis=0
            ).astype(BF16)
        return carry

    lax.fori_loop(0, 12, shifts, 0)

    for f in range(2):
        for half in range(2):
            turn(f, half, 1)
        for half in range(2):
            end(f, half, 1)

    gs = take(N_G)
    for d in range(1, 16):
        to = lax.rem(r + d, 16)
        send(gsum, gall.at[r], gs + d - 1, (s, to))
    gall[r] = gsum[...]

    def load_chunk(f, n):
        for k, (a, b, cc, d, u), count in runs_of(n):
            wbuf[k : k + count] = filt[f, a, b, cc, d, u : u + count]

    from_sib(0)
    y_at = 1 - by
    for n in range(9):
        a, b = divmod(n, 3)
        load_chunk(0, n)

        def one(i, carry, a=a, b=b, n=n):
            lhs = field[pl.ds(2 * i + a, 2), pl.ds(y_at + b, 5)].reshape(240, 768)
            part = jnp.dot(lhs, wbuf[...].reshape(768, 256), preferred_element_type=F32)
            rows = pl.ds(2 * i, 2)
            part = part.reshape(2, 5, 24, 256)
            acc[rows] = part if n == 0 else acc[rows] + part
            return carry

        lax.fori_loop(0, 5, one, 0)

    def activate(i, carry):
        ok = (i + 8 * bx >= 1) & (i + 8 * bx < 65)
        low = bz == 0
        hid[i, 5 * by] = jnp.zeros((16, 768), BF16)
        for j in range(5):
            h = jnp.where(ok, gelu(acc[i, j]), 0.0)
            none = jnp.zeros((1, 256), F32)
            edge = h[16:17]
            hid[i, y_at + j, :, 0:256] = jnp.concatenate(
                [jnp.where(low, none, edge), h[0:15]], axis=0
            ).astype(BF16)
            hid[i, y_at + j, :, 256:512] = h[0:16].astype(BF16)
            hid[i, y_at + j, :, 512:768] = jnp.concatenate(
                [h[1:16], jnp.where(low, edge, none)], axis=0
            ).astype(BF16)
        return carry

    lax.fori_loop(0, 10, activate, 0)

    from_sib(1)
    for n in range(9):
        a, b = divmod(n, 3)
        load_chunk(1, n)

        def two(i, carry, a=a, b=b, n=n):
            lhs = hid[pl.ds(4 * i + a, 4), b : b + 4].reshape(256, 768)
            part = jnp.dot(lhs, wbuf[...].reshape(768, 256), preferred_element_type=F32)
            rows = pl.ds(4 * i, 4)
            part = part.reshape(4, 4, 16, 256)
            acc[rows, 0:4, 0:16] = part if n == 0 else acc[rows, 0:4, 0:16] + part
            return carry

        lax.fori_loop(0, 2, two, 0)

    def finish(i, carry):
        feat[i] = gelu(acc[i, 0:4, 0:16]).astype(BF16)
        return carry

    lax.fori_loop(0, 8, finish, 0)

    for d in range(1, 16):
        arrived(gall.at[lax.rem(r + 16 - d, 16)], gs + d - 1)
    for f in range(2):
        owned = owner[f, s] == r
        for d in range(16):
            dl, dx, dc = d // 8, d // 2 % 4, d % 2
            for u in range(2):
                at = 7 * (2 * dc + dl) + 2 * dx + u
                if 2 * dx + u > 6 or at >= UNITS:
                    continue
                g = gall[d, f, u].astype(F32)
                m, v = mom1[f, at], mom2[f, at]
                mom1_out[f, at] = jnp.where(owned, 0.9 * m + 0.1 * g, m)
                mom2_out[f, at] = jnp.where(owned, 0.95 * v + 0.05 * (g * g), v)
                pan[f, at] = filt[f, yhi, z, dc, dl, 2 * dx + u]
    for copy in sent:
        copy.wait_send()


def shards(volumes, grad_parts, master, mom1, mom2, owner):
    def units(a):
        return a.reshape(2, UNITS, 8, 256)

    vmem = pl.BlockSpec(memory_space=pltpu.VMEM)
    n_sems = N_A2A + N_HALO + N_Z + N_RING + N_SIB + N_G
    state = jax.ShapeDtypeStruct((2, UNITS, 8, 256), F32)
    feat, pan, m_out, v_out = pl.pallas_call(
        body,
        out_shape=(
            jax.ShapeDtypeStruct((8, 4, 16, 256), BF16),
            jax.ShapeDtypeStruct((2, UNITS, 8, 256), BF16),
            state,
            state,
        ),
        in_specs=[pl.BlockSpec(memory_space=pltpu.SMEM)] + [vmem] * 5,
        out_specs=[vmem] * 4,
        scratch_shapes=[
            pltpu.VMEM((16, 2, 3, 2, 8, 256), BF16),
            pltpu.VMEM((16, 2, 3, 2, 8, 256), BF16),
            pltpu.VMEM((2, 2, 8, 256), BF16),
            pltpu.VMEM((16, 2, 2, 8, 256), BF16),
            pltpu.VMEM((2, 2, ZS, 2, 2, 8, 8, 256), BF16),
            pltpu.VMEM((12, 8, 16, 256), BF16),
            pltpu.VMEM((12, 16, 256), BF16),
            pltpu.VMEM((12, 16, 256), BF16),
            pltpu.VMEM((12, 8, 24, 768), BF16),
            pltpu.VMEM((10, 5, 24, 256), F32),
            pltpu.VMEM((10, 6, 16, 768), BF16),
            pltpu.VMEM((96, 8, 256), BF16),
            pltpu.SemaphoreType.DMA((n_sems,)),
            pltpu.SemaphoreType.DMA((n_sems,)),
        ],
        compiler_params=pltpu.CompilerParams(
            collective_id=0, has_side_effects=True, vmem_limit_bytes=56 << 20
        ),
    )(owner, volumes[0, 0], units(grad_parts[0]), units(master), units(mom1[0]), units(mom2[0]))
    share = lax.dynamic_slice_in_dim(
        pan.reshape(2, UNITS * 2048), lax.axis_index("rep") * 3456, 3456, 1
    ).astype(F32)
    return (
        feat[None, None],
        share,
        m_out.reshape(1, 2, 216, 256),
        v_out.reshape(1, 2, 216, 256),
    )


def solution(mesh):
    placed = (
        P("rep", "space", None, None, None, None),
        P("rep", None, "space", None),
        P(None, "space", None),
        P("rep", None, "space", None),
        P("rep", None, "space", None),
        P(),
    )
    return jax.shard_map(
        shards,
        mesh=mesh,
        in_specs=placed,
        out_specs=(
            P("rep", "space", None, None, None, None),
            P(None, ("space", "rep")),
            P("rep", None, "space", None),
            P("rep", None, "space", None),
        ),
        check_vma=False,
    )
```

```python
import jax
import jax.numpy as jnp
from jax import lax
from jax.experimental import pallas as pl
from jax.experimental.pallas import tpu as pltpu
from jax.sharding import PartitionSpec as P

MESH = pl.DeviceIdType.MESH
F32 = jnp.float32
BF16 = jnp.bfloat16
UNITS = 27
ZS = 16
NX = 5
N_A2A, N_HALO, N_RING, N_SIB, N_G = 7, 6, 48, 24, 8


def unit_of(row_unit):
    panel, within = divmod(row_unit, UNITS)
    group, place = divmod(within, 7)
    return panel // ZS, panel % ZS, group // 2, group % 2, place


def runs_of(chunk):
    runs = []
    for k in range(96):
        at = unit_of(96 * chunk + k)
        if runs and runs[-1][1][:4] == at[:4] and runs[-1][1][4] + runs[-1][2] == at[4]:
            runs[-1][2] += 1
        else:
            runs.append([k, at, 1])
    return runs


def gelu(v):
    return 0.5 * v * (1.0 + jnp.tanh(0.7978845608028654 * (v + 0.044715 * (v * v * v))))


def body(
    owner, vol, grads, master, mom1, mom2,
    conv, pan, sums,
    stage, paired, got, gsum, gall, filt, raw, edge_out, edge_in, field, acc, hid, wbuf,
    bar_send, bar_recv,
):
    s = lax.axis_index("space")
    r = lax.axis_index("rep")
    yhi, z = s // ZS, lax.rem(s, ZS)
    ylo, x, c = r // 8, lax.rem(r // 2, 4), lax.rem(r, 2)
    y = 2 * yhi + ylo
    bx, by, bz = s // 4, lax.rem(s // 2, 2), lax.rem(s, 2)

    def device(px, py, pz, pc):
        return (py // 2 * ZS + pz, lax.rem(py, 2) * 8 + 2 * px + pc)

    q = 4 * ylo + x
    xp, xm, xo = lax.rem(x + 1, 4), lax.rem(x + 3, 4), lax.rem(x + 2, 4)
    yp, ym, yo = lax.rem(y + 1, 4), lax.rem(y + 3, 4), lax.rem(y + 2, 4)
    zh, zl = z // 4, lax.rem(z, 4)
    lp, lm, lo = lax.rem(zl + 1, 4), lax.rem(zl + 3, 4), lax.rem(zl + 2, 4)

    def along_z(n):
        return device(x, y, lax.rem(z + n + ZS, ZS), c)

    sib_dev = device(x, y, z, 1 - c)
    other_y = jnp.where(ylo == 0, ym, yp)

    def chip(n):
        return (s, 2 * n + c)

    flip = 2 - 4 * by
    halo_peers = []
    for dx, fl in ((-1, 0), (1, 0), (0, 1), (-1, 1), (1, 1)):
        halo_peers.append((dx, fl, (lax.rem(s + fl * flip + 4 * dx + 32, 32), r)))

    barrier = pltpu.get_barrier_semaphore()
    all_peers = [sib_dev] + [chip(lax.rem(q + d, 8)) for d in range(1, 8)]
    all_peers += [along_z(n) for n in (4, -4, 8, 1, -1, 2, -2)] + [device(x, other_y, z, c)]
    all_peers += [p for _, _, p in halo_peers]
    for p in all_peers:
        pl.semaphore_signal(barrier, inc=1, device_id=p, device_id_type=MESH)

    for d in range(16):
        dc, dl, dx = d // 8, d // 4 % 2, d % 4
        first = 7 * (2 * dc + dl) + 2 * dx
        for u in range(2):
            at = min(first + (u if dx < 3 else 0), UNITS - 1)
            stage[dc, d % 8, :, 0, u] = grads[:, at]
            stage[dc, d % 8, :, 1, u] = mom1[:, at].astype(BF16)
            stage[dc, d % 8, :, 2, u] = mom2[:, at].astype(BF16)

    pl.semaphore_wait(barrier, len(all_peers))

    sent = []
    base = [0]

    def take(n):
        base[0] += n
        return base[0] - n

    def send(src, dst, k, dev):
        copy = pltpu.make_async_remote_copy(
            src_ref=src, dst_ref=dst, send_sem=bar_send.at[k], recv_sem=bar_recv.at[k],
            device_id=dev, device_id_type=MESH,
        )
        copy.start()
        sent.append(copy)

    def arrived(dst, k):
        pltpu.make_async_remote_copy(
            src_ref=dst, dst_ref=dst, send_sem=bar_send.at[k], recv_sem=bar_recv.at[k],
            device_id=(s, r), device_id_type=MESH,
        ).wait_recv()

    pair = take(1)
    send(stage.at[1 - c], paired, pair, sib_dev)
    halo = take(N_HALO)
    x_src = {-1: (0, 2), 0: (0, 8), 1: (6, 2)}
    x_dst = {-1: 10, 0: 2, 1: 0}
    for k, (dx, fl, dev) in enumerate(halo_peers):
        sx, nx = x_src[dx]
        sy, dy, ny = (2 * (1 - by), 6 * by, 2) if fl else (0, 2, 4)
        send(
            vol.at[pl.ds(sx, nx), pl.ds(sy, ny)],
            raw.at[pl.ds(x_dst[dx], nx), pl.ds(dy, ny)],
            halo + k, dev,
        )

    arrived(paired, pair)
    a2a = take(N_A2A)
    sib_owns = [owner[f, s] == 2 * q + 1 - c for f in range(2)]
    for d in range(1, 9):
        to = lax.rem(q + d, 8)
        for f in range(2):
            g = stage[c, to, f, 0].astype(F32) + paired[to, f, 0].astype(F32)
            stage[c, to, f, 0] = g.astype(BF16)
            for k in (1, 2):
                mine, other = stage[c, to, f, k], paired[to, f, k]
                stage[c, to, f, k] = jnp.where(sib_owns[f], other.astype(F32), mine.astype(F32)).astype(BF16)
        if d < 8:
            send(stage.at[c, to], got.at[q], a2a + d - 1, chip(to))
    got[q] = stage[c, q]
    raw[2:10, 2:6] = vol[...]

    for d in range(1, 8):
        arrived(got.at[lax.rem(q + 8 - d, 8)], a2a + d - 1)
    first = 7 * (2 * c + ylo) + 2 * x
    corr_one = 1.0 - 0.9**10
    corr_two = 1.0 - 0.95**10
    for f in range(2):
        own = owner[f, s] // 2
        for u in range(2):
            total = got[0, f, 0, u].astype(F32)
            for k in range(1, 8):
                total = total + got[k, f, 0, u].astype(F32)
            m_new = 0.9 * got[own, f, 1, u].astype(F32) + 0.1 * total
            v_new = 0.95 * got[own, f, 2, u].astype(F32) + 0.05 * (total * total)
            w = master[f, jnp.minimum(first + u, UNITS - 1)]
            step = m_new / corr_one / (jnp.sqrt(v_new / corr_two) + 1e-08) + 0.1 * w
            gsum[f, u] = total.astype(BF16)
            filt[f, yhi, 0, 0, c, ylo, 2 * x + u] = (w - 0.004 * step).astype(BF16)

    mine = pl.ds(2 * x, 2)

    def blk(off, k):
        return filt.at[:, yhi, off, k, c, ylo, mine]

    far = take(3)
    send(blk(0, 0), blk(3, 0), far, along_z(4))
    send(blk(0, 0), blk(1, 0), far + 1, along_z(-4))
    send(blk(0, 0), blk(2, 0), far + 2, along_z(8))
    near = {off: take(3) for off in (0, 3, 2)}

    def send_near(off):
        send(blk(off, 0), blk(off, 3), near[off], along_z(1))
        send(blk(off, 0), blk(off, 1), near[off] + 1, along_z(-1))
        send(blk(off, 0), blk(off, 2), near[off] + 2, along_z(2 - 4 * yhi))

    def wait_near(off):
        for n, k in enumerate((3, 1, 2)):
            arrived(blk(off, k), near[off] + n)

    side = take(3)

    def side_block(pos):
        return filt.at[:, yhi, 1, 0, c, ylo, pl.ds(2 * pos, 2)]

    kinds = {
        (0, 0): 1, (1, 0): 0, (0, 3): 0, (1, 3): 1, (0, 2): 1, (1, 2): 0, (0, 1): 2, (1, 1): 2,
    }
    ring = take(N_RING + 16)
    sib = take(N_SIB + 8)
    ways = {
        "x": (x, xp, xm, xo, device(xp, y, z, c), device(xm, y, z, c)),
        "y": (y, yp, ym, yo, device(x, yp, z, c), device(x, ym, z, c)),
        "z": (0, 1, 3, 2, along_z(1), along_z(-1)),
    }
    order = {0: "yx", 1: "xy", 2: "yz"}

    def ring_of(f, off, phase):
        n = ring + 4 * (8 * f + 2 * off + phase)
        kind = kinds[f, off]

        def reg(pos, half=None, core=c):
            if kind == 2:
                if phase == 0:
                    u0, nu = {None: (0, 7), 0: (0, 4), 1: (4, 3)}[half]
                    return filt.at[f, pos // 2, off, 0, core, lax.rem(pos, 2), pl.ds(u0, nu)]
                hi = pl.ds(0, 2) if half is None else pl.ds(half, 1)
                return filt.at[f, hi, off, pos, core, :, pl.ds(0, 7)]
            ks = pl.ds(0, 4) if half is None else pl.ds(2 * half, 2)
            if kind == 0 and phase == 0:
                return filt.at[f, pos // 2, off, ks, core, lax.rem(pos, 2), mine]
            if kind == 0:
                hi = pl.ds(0, 2) if half is None else pl.ds(half, 1)
                return filt.at[f, hi, off, :, core, :, pl.ds(2 * pos, 2)]
            if phase == 0:
                return filt.at[f, yhi, off, ks, core, ylo, pl.ds(2 * pos, 2)]
            return filt.at[f, pos // 2, off, ks, core, lax.rem(pos, 2), pl.ds(0, 7)]

        return (n, order[kind][phase] == "z") + ways[order[kind][phase]] + (reg,)

    def start(f, off, phase):
        n, rel, me, plus, minus, opp, to_plus, to_minus, reg = ring_of(f, off, phase)
        send(reg(me), reg(minus if rel else me), n, to_plus)
        send(reg(me), reg(plus if rel else me), n + 1, to_minus)
        if phase == 1:
            send(reg(me), reg(me), sib + 4 * (4 * f + off), sib_dev)

    def turn(f, off, phase):
        n, rel, me, plus, minus, opp, to_plus, to_minus, reg = ring_of(f, off, phase)
        arrived(reg(minus), n)
        send(reg(minus, 0), reg(opp if rel else minus, 0), n + 2, to_plus)
        arrived(reg(plus), n + 1)
        send(reg(plus, 1), reg(opp if rel else plus, 1), n + 3, to_minus)
        if phase == 1:
            m = sib + 4 * (4 * f + off)
            send(reg(minus), reg(minus), m + 1, sib_dev)
            send(reg(plus), reg(plus), m + 2, sib_dev)

    def end(f, off, phase):
        n, rel, me, plus, minus, opp, to_plus, to_minus, reg = ring_of(f, off, phase)
        arrived(reg(opp, 0), n + 2)
        arrived(reg(opp, 1), n + 3)
        if phase == 1:
            send(reg(opp), reg(opp), sib + 4 * (4 * f + off) + 3, sib_dev)

    def from_sib(f):
        for off in range(4):
            n, rel, me, plus, minus, opp, to_plus, to_minus, reg = ring_of(f, off, 1)
            for m, pos in enumerate((me, minus, plus, opp)):
                arrived(reg(pos, None, 1 - c), sib + 4 * (4 * f + off) + m)

    send_near(0)
    wait_near(0)
    start(0, 0, 0)
    start(1, 0, 0)
    arrived(blk(3, 0), far)
    send_near(3)
    arrived(blk(1, 0), far + 1)
    for n, pos in enumerate((xp, xm, xo)):
        send(side_block(x), side_block(x), side + n, device(pos, y, z, c))
    arrived(blk(2, 0), far + 2)
    send_near(2)
    turn(0, 0, 0)
    turn(1, 0, 0)
    wait_near(3)
    start(0, 3, 0)
    start(1, 3, 0)
    for n, pos in enumerate((xm, xp, xo)):
        arrived(side_block(pos), side + n)
    start(0, 1, 0)
    start(1, 1, 0)

    for k, (dx, fl, dev) in enumerate(halo_peers):
        sx, nx = x_src[dx]
        dy, ny = (6 * (1 - by), 2) if fl else (2, 4)
        dst_x = {-1: 0, 0: 2, 1: 10}[dx]
        pairs = raw.at[pl.ds(dst_x, nx), pl.ds(dy, ny)]
        arrived(pairs, halo + {0: 1, 1: 0, 2: 2, 3: 4, 4: 3}[k])

    def pack(i, carry):
        rows = [raw[i, j].astype(F32) for j in range(8)]
        near = jnp.concatenate([jnp.where(bz == 0, v[15:16], v[0:1]) for v in rows], axis=0)
        far = jnp.concatenate([jnp.where(bz == 0, v[14:15], v[1:2]) for v in rows], axis=0)
        edge_out[i] = jnp.concatenate([near, far], axis=0).astype(BF16)
        return carry

    lax.fori_loop(0, 12, pack, 0)
    z_partner = z + 1 - 2 * bz
    send(edge_out, edge_in, halo + 5, device(x, y, z_partner, c))

    end(0, 0, 0)
    start(0, 0, 1)
    wait_near(2)
    start(0, 2, 0)
    start(1, 2, 0)
    turn(0, 3, 0)
    turn(0, 1, 0)
    turn(1, 3, 0)
    turn(1, 1, 0)
    end(1, 0, 0)
    end(0, 3, 0)
    start(0, 3, 1)
    turn(0, 2, 0)
    turn(1, 2, 0)
    end(0, 1, 0)
    start(0, 1, 1)
    end(0, 2, 0)
    start(0, 2, 1)
    turn(0, 0, 1)
    start(1, 0, 1)
    for off in (3, 1, 2):
        end(1, off, 0)
        start(1, off, 1)

    gs = take(N_G)
    for d in range(1, 8):
        to = lax.rem(q + d, 8)
        send(gsum, gall.at[c, q], gs + d - 1, chip(to))
    gall[c, q] = gsum[...]

    arrived(edge_in, halo + 5)

    def shifts(i, carry):
        edges = edge_in[i].astype(F32)
        x_ok = (i + 8 * bx >= 2) & (i + 8 * bx < 66)
        for j in range(8):
            y_ok = (j + 4 * by >= 2) & (j + 4 * by < 10)
            ok = x_ok & y_ok
            v = jnp.where(ok, raw[i, j].astype(F32), 0.0)
            e0 = jnp.where(ok, edges[j : j + 1], 0.0)
            e1 = jnp.where(ok, edges[8 + j : 9 + j], 0.0)
            none = jnp.zeros((1, 256), F32)
            rest = jnp.zeros((7, 256), F32)
            low = bz == 0
            field[i, j, :, 0:256] = jnp.concatenate(
                [jnp.where(low, none, e0), v[0:15], jnp.where(low, v[15:16], e1), rest], axis=0
            ).astype(BF16)
            field[i, j, :, 256:512] = jnp.concatenate([v, e0, rest], axis=0).astype(BF16)
            field[i, j, :, 512:768] = jnp.concatenate(
                [v[1:16], jnp.where(low, e0, none), jnp.where(low, e1, v[0:1]), rest], axis=0
            ).astype(BF16)
        return carry

    lax.fori_loop(0, 12, shifts, 0)

    for off in (3, 1, 2):
        turn(0, off, 1)
    end(0, 0, 1)
    turn(1, 0, 1)
    turn(1, 3, 1)
    for off in (3, 1, 2):
        end(0, off, 1)
    from_sib(0)

    def load_chunk(f, n):
        for at, (a, b, cc, d, u), count in runs_of(n):
            k = lax.rem(b - z + ZS, 4)
            step = k - 4 * (k // (2 + a))
            off = lax.rem(b - z - step + 2 * ZS, ZS) // 4
            wbuf[at : at + count] = filt[f, a, off, k, cc, d, u : u + count]

    y_at = 1 - by

    def first_conv(n):
        a, b = divmod(n, 3)
        load_chunk(0, n)

        def one(i, carry):
            lhs = field[pl.ds(NX * i + a, NX), pl.ds(y_at + b, 5)].reshape(NX * 120, 768)
            part = jnp.dot(lhs, wbuf[...].reshape(768, 256), preferred_element_type=F32)
            rows = pl.ds(NX * i, NX)
            part = part.reshape(NX, 5, 24, 256)
            acc[rows] = part if n == 0 else acc[rows] + part
            return carry

        lax.fori_loop(0, 10 // NX, one, 0)

    first_conv(0)
    first_conv(1)
    turn(1, 1, 1)
    turn(1, 2, 1)
    for n in range(2, 5):
        first_conv(n)
    for off in (0, 3, 1, 2):
        end(1, off, 1)
    for d in range(1, 8):
        arrived(gall.at[c, lax.rem(q + 8 - d, 8)], gs + d - 1)
    send(gall.at[c], gall.at[c], gs + 7, sib_dev)
    for n in range(5, 9):
        first_conv(n)

    def activate(i, carry):
        ok = (i + 8 * bx >= 1) & (i + 8 * bx < 65)
        low = bz == 0
        hid[i, 5 * by] = jnp.zeros((16, 768), BF16)
        for j in range(5):
            h = jnp.where(ok, gelu(acc[i, j]), 0.0)
            none = jnp.zeros((1, 256), F32)
            edge = h[16:17]
            hid[i, y_at + j, :, 0:256] = jnp.concatenate(
                [jnp.where(low, none, edge), h[0:15]], axis=0
            ).astype(BF16)
            hid[i, y_at + j, :, 256:512] = h[0:16].astype(BF16)
            hid[i, y_at + j, :, 512:768] = jnp.concatenate(
                [h[1:16], jnp.where(low, edge, none)], axis=0
            ).astype(BF16)
        return carry

    lax.fori_loop(0, 10, activate, 0)

    from_sib(1)
    for n in range(9):
        a, b = divmod(n, 3)
        load_chunk(1, n)
        lhs = hid[a : a + 8, b : b + 4].reshape(512, 768)
        part = jnp.dot(lhs, wbuf[...].reshape(768, 256), preferred_element_type=F32)
        part = part.reshape(8, 4, 16, 256)
        conv[...] = part if n == 0 else conv[...] + part

    arrived(gall.at[1 - c], gs + 7)
    sums[...] = gall[...]
    for f in range(2):
        for g in range(4):
            n = min(7, UNITS - 7 * g)
            pan[f, 7 * g : 7 * g + n] = filt[f, yhi, 0, 0, g // 2, g % 2, 0:n]
    for copy in sent:
        copy.wait_send()


def outputs(owned, conv, gall, mom1, mom2, feat, mom1_out, mom2_out):
    def finish(i, carry):
        feat[i] = gelu(conv[i]).astype(BF16)
        return carry

    lax.fori_loop(0, 8, finish, 0)
    for f in range(2):
        here = owned[f] == 1
        for d in range(16):
            dc, dl, dx = d // 8, d // 4 % 2, d % 4
            for u in range(2):
                at = 7 * (2 * dc + dl) + 2 * dx + u
                if 2 * dx + u > 6 or at >= UNITS:
                    continue
                g = gall[dc, d % 8, f, u].astype(F32)
                m, v = mom1[f, at], mom2[f, at]
                mom1_out[f, at] = jnp.where(here, 0.9 * m + 0.1 * g, m)
                mom2_out[f, at] = jnp.where(here, 0.95 * v + 0.05 * (g * g), v)


def shards(volumes, grad_parts, master, mom1, mom2, owner):
    def units(a):
        return a.reshape(2, UNITS, 8, 256)

    vmem = pl.BlockSpec(memory_space=pltpu.VMEM)
    n_sems = 16 + N_A2A + N_HALO + N_RING + 16 + N_SIB + 8 + N_G
    state = jax.ShapeDtypeStruct((2, UNITS, 8, 256), F32)
    smem = pl.BlockSpec(memory_space=pltpu.SMEM)
    args = (units(mom1[0]), units(mom2[0]))
    conv, pan, gall = pl.pallas_call(
        body,
        out_shape=(
            jax.ShapeDtypeStruct((8, 4, 16, 256), F32),
            jax.ShapeDtypeStruct((2, UNITS, 8, 256), BF16),
            jax.ShapeDtypeStruct((2, 8, 2, 2, 8, 256), BF16),
        ),
        in_specs=[smem] + [vmem] * 5,
        out_specs=[vmem] * 3,
        scratch_shapes=[
            pltpu.VMEM((2, 8, 2, 3, 2, 8, 256), BF16),
            pltpu.VMEM((8, 2, 3, 2, 8, 256), BF16),
            pltpu.VMEM((8, 2, 3, 2, 8, 256), BF16),
            pltpu.VMEM((2, 2, 8, 256), BF16),
            pltpu.VMEM((2, 8, 2, 2, 8, 256), BF16),
            pltpu.VMEM((2, 2, 4, 4, 2, 2, 8, 8, 256), BF16),
            pltpu.VMEM((12, 8, 16, 256), BF16),
            pltpu.VMEM((12, 16, 256), BF16),
            pltpu.VMEM((12, 16, 256), BF16),
            pltpu.VMEM((12, 8, 24, 768), BF16),
            pltpu.VMEM((10, 5, 24, 256), F32),
            pltpu.VMEM((10, 6, 16, 768), BF16),
            pltpu.VMEM((96, 8, 256), BF16),
            pltpu.SemaphoreType.DMA((n_sems,)),
            pltpu.SemaphoreType.DMA((n_sems,)),
        ],
        compiler_params=pltpu.CompilerParams(
            collective_id=0, has_side_effects=True, vmem_limit_bytes=56 << 20
        ),
    )(owner, volumes[0, 0], units(grad_parts[0]), units(master), *args)
    s, r = lax.axis_index("space"), lax.axis_index("rep")
    owned = (lax.dynamic_slice_in_dim(owner, s, 1, 1)[:, 0] == r).astype(jnp.int32)
    feat, m_out, v_out = pl.pallas_call(
        outputs,
        out_shape=(jax.ShapeDtypeStruct((8, 4, 16, 256), BF16), state, state),
        in_specs=[smem] + [vmem] * 4,
        out_specs=[vmem] * 3,
        compiler_params=pltpu.CompilerParams(vmem_limit_bytes=16 << 20),
    )(owned, conv, gall, *args)
    rows = lax.dynamic_slice_in_dim(pan.reshape(2, 216, 256), 27 * (r // 2), 27, 1)
    rows = rows.astype(F32).reshape(2, 2, 3456)
    share = lax.dynamic_index_in_dim(rows, lax.rem(r, 2), 1, keepdims=False)
    return (
        feat[None, None],
        share,
        m_out.reshape(1, 2, 216, 256),
        v_out.reshape(1, 2, 216, 256),
    )


def solution(mesh):
    placed = (
        P("rep", "space", None, None, None, None),
        P("rep", None, "space", None),
        P(None, "space", None),
        P("rep", None, "space", None),
        P("rep", None, "space", None),
        P(),
    )
    return jax.shard_map(
        shards,
        mesh=mesh,
        in_specs=placed,
        out_specs=(
            P("rep", "space", None, None, None, None),
            P(None, ("space", "rep")),
            P("rep", None, "space", None),
            P("rep", None, "space", None),
        ),
        check_vma=False,
    )
```

```python
import jax
import jax.numpy as jnp
from jax import lax
from jax.experimental import pallas as pl
from jax.experimental.pallas import tpu as pltpu
from jax.sharding import PartitionSpec as P

MESH = pl.DeviceIdType.MESH
F32 = jnp.float32
BF16 = jnp.bfloat16
UNITS = 27
ZS = 16
NX = 5
N_A2A, N_HALO, N_RING, N_SIB, N_G = 7, 6, 48, 24, 8

PLAN = (
    ("near", 0, 0), ("far", 0, 1), ("far", 0, 3), ("turn0", 0, 0), ("turn0", 1, 0), ("side", 0, 1), ("end0", 0, 0),
    ("far", 0, 2), ("near", 0, 3), ("turn0", 0, 1), ("turn0", 1, 1), ("turn0", 1, 3), ("near", 0, 2), ("edges",),
    ("end0", 1, 0), ("turn1", 0, 0), ("turn0", 0, 3), ("turn0", 1, 2), ("turn0", 0, 2), ("end1", 0, 0),
    ("end0", 0, 3), ("end0", 0, 1), ("end0", 1, 3), ("end0", 0, 2), ("turn1", 1, 0), ("end0", 1, 1), ("turn1", 0, 3),
    ("turn1", 0, 1), ("shift",), ("end0", 1, 2), ("sums",), ("turn1", 0, 2), ("end1", 0, 1), ("end1", 0, 3),
    ("turn1", 1, 3), ("turn1", 1, 1), ("end1", 0, 2), ("end1", 1, 0), ("turn1", 1, 2), ("sib", 0), ("conv", 0),
    ("conv", 1), ("end1", 1, 3), ("end1", 1, 1), ("end1", 1, 2), ("conv", 2), ("conv", 3), ("conv", 4), ("gs",),
    ("conv", 5), ("conv", 6), ("conv", 7), ("conv", 8),
)


def unit_of(row_unit):
    panel, within = divmod(row_unit, UNITS)
    group, place = divmod(within, 7)
    return panel // ZS, panel % ZS, group // 2, group % 2, place


def runs_of(chunk):
    runs = []
    for k in range(96):
        at = unit_of(96 * chunk + k)
        if runs and runs[-1][1][:4] == at[:4] and runs[-1][1][4] + runs[-1][2] == at[4]:
            runs[-1][2] += 1
        else:
            runs.append([k, at, 1])
    return runs


def gelu(v):
    return 0.5 * v * (1.0 + jnp.tanh(0.7978845608028654 * (v + 0.044715 * (v * v * v))))


def body(
    owner, vol, grads, master, mom1, mom2,
    conv, pan, sums,
    stage, paired, got, gsum, gall, filt, raw, edge_out, edge_in, field, acc, hid, wbuf,
    bar_send, bar_recv,
):
    s = lax.axis_index("space")
    r = lax.axis_index("rep")
    yhi, z = s // ZS, lax.rem(s, ZS)
    ylo, x, c = r // 8, lax.rem(r // 2, 4), lax.rem(r, 2)
    y = 2 * yhi + ylo
    bx, by, bz = s // 4, lax.rem(s // 2, 2), lax.rem(s, 2)

    def device(px, py, pz, pc):
        return (py // 2 * ZS + pz, lax.rem(py, 2) * 8 + 2 * px + pc)

    q = 4 * ylo + x
    xp, xm, xo = lax.rem(x + 1, 4), lax.rem(x + 3, 4), lax.rem(x + 2, 4)
    yp, ym, yo = lax.rem(y + 1, 4), lax.rem(y + 3, 4), lax.rem(y + 2, 4)
    zh, zl = z // 4, lax.rem(z, 4)
    lp, lm, lo = lax.rem(zl + 1, 4), lax.rem(zl + 3, 4), lax.rem(zl + 2, 4)

    def along_z(n):
        return device(x, y, lax.rem(z + n + ZS, ZS), c)

    sib_dev = device(x, y, z, 1 - c)
    other_y = jnp.where(ylo == 0, ym, yp)

    def chip(n):
        return (s, 2 * n + c)

    flip = 2 - 4 * by
    halo_peers = []
    for dx, fl in ((-1, 0), (1, 0), (0, 1), (-1, 1), (1, 1)):
        halo_peers.append((dx, fl, (lax.rem(s + fl * flip + 4 * dx + 32, 32), r)))

    barrier = pltpu.get_barrier_semaphore()
    all_peers = [sib_dev] + [chip(lax.rem(q + d, 8)) for d in range(1, 8)]
    all_peers += [along_z(n) for n in (4, -4, 8, 1, -1, 2, -2)] + [device(x, other_y, z, c)]
    all_peers += [p for _, _, p in halo_peers]
    for p in all_peers:
        pl.semaphore_signal(barrier, inc=1, device_id=p, device_id_type=MESH)

    for d in range(16):
        dc, dl, dx = d // 8, d // 4 % 2, d % 4
        first = 7 * (2 * dc + dl) + 2 * dx
        for u in range(2):
            at = min(first + (u if dx < 3 else 0), UNITS - 1)
            stage[dc, d % 8, :, 0, u] = grads[:, at]
            stage[dc, d % 8, :, 1, u] = mom1[:, at].astype(BF16)
            stage[dc, d % 8, :, 2, u] = mom2[:, at].astype(BF16)

    pl.semaphore_wait(barrier, len(all_peers))

    sent = []
    base = [0]

    def take(n):
        base[0] += n
        return base[0] - n

    def send(src, dst, k, dev):
        copy = pltpu.make_async_remote_copy(
            src_ref=src, dst_ref=dst, send_sem=bar_send.at[k], recv_sem=bar_recv.at[k],
            device_id=dev, device_id_type=MESH,
        )
        copy.start()
        sent.append(copy)

    def arrived(dst, k):
        pltpu.make_async_remote_copy(
            src_ref=dst, dst_ref=dst, send_sem=bar_send.at[k], recv_sem=bar_recv.at[k],
            device_id=(s, r), device_id_type=MESH,
        ).wait_recv()

    pair = take(1)
    send(stage.at[1 - c], paired, pair, sib_dev)
    halo = take(N_HALO)
    x_src = {-1: (0, 2), 0: (0, 8), 1: (6, 2)}
    x_dst = {-1: 10, 0: 2, 1: 0}
    for k, (dx, fl, dev) in enumerate(halo_peers):
        sx, nx = x_src[dx]
        sy, dy, ny = (2 * (1 - by), 6 * by, 2) if fl else (0, 2, 4)
        send(
            vol.at[pl.ds(sx, nx), pl.ds(sy, ny)],
            raw.at[pl.ds(x_dst[dx], nx), pl.ds(dy, ny)],
            halo + k, dev,
        )

    arrived(paired, pair)
    a2a = take(N_A2A)
    sib_owns = [owner[f, s] == 2 * q + 1 - c for f in range(2)]
    for d in range(1, 9):
        to = lax.rem(q + d, 8)
        for f in range(2):
            g = stage[c, to, f, 0].astype(F32) + paired[to, f, 0].astype(F32)
            stage[c, to, f, 0] = g.astype(BF16)
            for k in (1, 2):
                mine, other = stage[c, to, f, k], paired[to, f, k]
                stage[c, to, f, k] = jnp.where(sib_owns[f], other.astype(F32), mine.astype(F32)).astype(BF16)
        if d < 8:
            send(stage.at[c, to], got.at[q], a2a + d - 1, chip(to))
    got[q] = stage[c, q]
    raw[2:10, 2:6] = vol[...]

    for d in range(1, 8):
        arrived(got.at[lax.rem(q + 8 - d, 8)], a2a + d - 1)
    first = 7 * (2 * c + ylo) + 2 * x
    corr_one = 1.0 - 0.9**10
    corr_two = 1.0 - 0.95**10
    for f in range(2):
        own = owner[f, s] // 2
        for u in range(2):
            total = got[0, f, 0, u].astype(F32)
            for k in range(1, 8):
                total = total + got[k, f, 0, u].astype(F32)
            m_new = 0.9 * got[own, f, 1, u].astype(F32) + 0.1 * total
            v_new = 0.95 * got[own, f, 2, u].astype(F32) + 0.05 * (total * total)
            w = master[f, jnp.minimum(first + u, UNITS - 1)]
            step = m_new / corr_one / (jnp.sqrt(v_new / corr_two) + 1e-08) + 0.1 * w
            gsum[f, u] = total.astype(BF16)
            filt[f, yhi, 0, 0, c, ylo, 2 * x + u] = (w - 0.004 * step).astype(BF16)

    mine = pl.ds(2 * x, 2)

    def blk(off, k):
        return filt.at[:, yhi, off, k, c, ylo, mine]

    far = take(3)
    send(blk(0, 0), blk(3, 0), far, along_z(4))
    send(blk(0, 0), blk(1, 0), far + 1, along_z(-4))
    send(blk(0, 0), blk(2, 0), far + 2, along_z(8))
    near = {off: take(3) for off in (0, 3, 2)}

    def send_near(off):
        send(blk(off, 0), blk(off, 3), near[off], along_z(1))
        send(blk(off, 0), blk(off, 1), near[off] + 1, along_z(-1))
        send(blk(off, 0), blk(off, 2), near[off] + 2, along_z(2 - 4 * yhi))

    def wait_near(off):
        for n, k in enumerate((3, 1, 2)):
            arrived(blk(off, k), near[off] + n)

    side = take(3)

    def side_block(pos):
        return filt.at[:, yhi, 1, 0, c, ylo, pl.ds(2 * pos, 2)]

    kinds = {
        (0, 0): 1, (1, 0): 0, (0, 3): 0, (1, 3): 1, (0, 2): 1, (1, 2): 0, (0, 1): 2, (1, 1): 2,
    }
    ring = take(N_RING + 16)
    sib = take(N_SIB + 8)
    ways = {
        "x": (x, xp, xm, xo, device(xp, y, z, c), device(xm, y, z, c)),
        "y": (y, yp, ym, yo, device(x, yp, z, c), device(x, ym, z, c)),
        "z": (0, 1, 3, 2, along_z(1), along_z(-1)),
    }
    order = {0: "yx", 1: "xy", 2: "yz"}

    def ring_of(f, off, phase):
        n = ring + 4 * (8 * f + 2 * off + phase)
        kind = kinds[f, off]

        def reg(pos, half=None, core=c):
            if kind == 2:
                if phase == 0:
                    u0, nu = {None: (0, 7), 0: (0, 4), 1: (4, 3)}[half]
                    return filt.at[f, pos // 2, off, 0, core, lax.rem(pos, 2), pl.ds(u0, nu)]
                hi = pl.ds(0, 2) if half is None else pl.ds(half, 1)
                return filt.at[f, hi, off, pos, core, :, pl.ds(0, 7)]
            ks = pl.ds(0, 4) if half is None else pl.ds(2 * half, 2)
            if kind == 0 and phase == 0:
                return filt.at[f, pos // 2, off, ks, core, lax.rem(pos, 2), mine]
            if kind == 0:
                hi = pl.ds(0, 2) if half is None else pl.ds(half, 1)
                return filt.at[f, hi, off, :, core, :, pl.ds(2 * pos, 2)]
            if phase == 0:
                return filt.at[f, yhi, off, ks, core, ylo, pl.ds(2 * pos, 2)]
            return filt.at[f, pos // 2, off, ks, core, lax.rem(pos, 2), pl.ds(0, 7)]

        return (n, order[kind][phase] == "z") + ways[order[kind][phase]] + (reg,)

    def start(f, off, phase):
        n, rel, me, plus, minus, opp, to_plus, to_minus, reg = ring_of(f, off, phase)
        send(reg(me), reg(minus if rel else me), n, to_plus)
        send(reg(me), reg(plus if rel else me), n + 1, to_minus)
        if phase == 1:
            send(reg(me), reg(me), sib + 4 * (4 * f + off), sib_dev)

    def turn(f, off, phase):
        n, rel, me, plus, minus, opp, to_plus, to_minus, reg = ring_of(f, off, phase)
        arrived(reg(minus), n)
        send(reg(minus, 0), reg(opp if rel else minus, 0), n + 2, to_plus)
        arrived(reg(plus), n + 1)
        send(reg(plus, 1), reg(opp if rel else plus, 1), n + 3, to_minus)
        if phase == 1:
            m = sib + 4 * (4 * f + off)
            send(reg(minus), reg(minus), m + 1, sib_dev)
            send(reg(plus), reg(plus), m + 2, sib_dev)

    def end(f, off, phase):
        n, rel, me, plus, minus, opp, to_plus, to_minus, reg = ring_of(f, off, phase)
        arrived(reg(opp, 0), n + 2)
        arrived(reg(opp, 1), n + 3)
        if phase == 1:
            send(reg(opp), reg(opp), sib + 4 * (4 * f + off) + 3, sib_dev)

    def from_sib(f):
        for off in range(4):
            n, rel, me, plus, minus, opp, to_plus, to_minus, reg = ring_of(f, off, 1)
            for m, pos in enumerate((me, minus, plus, opp)):
                arrived(reg(pos, None, 1 - c), sib + 4 * (4 * f + off) + m)

    gs = take(N_G)

    def edges():
        for k, (dx, fl, dev) in enumerate(halo_peers):
            sx, nx = x_src[dx]
            dy, ny = (6 * (1 - by), 2) if fl else (2, 4)
            dst_x = {-1: 0, 0: 2, 1: 10}[dx]
            pairs = raw.at[pl.ds(dst_x, nx), pl.ds(dy, ny)]
            arrived(pairs, halo + {0: 1, 1: 0, 2: 2, 3: 4, 4: 3}[k])

        def pack(i, carry):
            rows = [raw[i, j].astype(F32) for j in range(8)]
            near = jnp.concatenate([jnp.where(bz == 0, v[15:16], v[0:1]) for v in rows], axis=0)
            far = jnp.concatenate([jnp.where(bz == 0, v[14:15], v[1:2]) for v in rows], axis=0)
            edge_out[i] = jnp.concatenate([near, far], axis=0).astype(BF16)
            return carry

        lax.fori_loop(0, 12, pack, 0)
        z_partner = z + 1 - 2 * bz
        send(edge_out, edge_in, halo + 5, device(x, y, z_partner, c))

    def send_sums():
        for d in range(1, 8):
            to = lax.rem(q + d, 8)
            send(gsum, gall.at[c, q], gs + d - 1, chip(to))
        gall[c, q] = gsum[...]

    def shift_field():
        arrived(edge_in, halo + 5)

        def shifts(i, carry):
            edges = edge_in[i].astype(F32)
            x_ok = (i + 8 * bx >= 2) & (i + 8 * bx < 66)
            for j in range(8):
                y_ok = (j + 4 * by >= 2) & (j + 4 * by < 10)
                ok = x_ok & y_ok
                v = jnp.where(ok, raw[i, j].astype(F32), 0.0)
                e0 = jnp.where(ok, edges[j : j + 1], 0.0)
                e1 = jnp.where(ok, edges[8 + j : 9 + j], 0.0)
                none = jnp.zeros((1, 256), F32)
                rest = jnp.zeros((7, 256), F32)
                low = bz == 0
                field[i, j, :, 0:256] = jnp.concatenate(
                    [jnp.where(low, none, e0), v[0:15], jnp.where(low, v[15:16], e1), rest], axis=0
                ).astype(BF16)
                field[i, j, :, 256:512] = jnp.concatenate([v, e0, rest], axis=0).astype(BF16)
                field[i, j, :, 512:768] = jnp.concatenate(
                    [v[1:16], jnp.where(low, e0, none), jnp.where(low, e1, v[0:1]), rest], axis=0
                ).astype(BF16)
            return carry

        lax.fori_loop(0, 12, shifts, 0)

    def load_chunk(f, n):
        for at, (a, b, cc, d, u), count in runs_of(n):
            k = lax.rem(b - z + ZS, 4)
            step = k - 4 * (k // (2 + a))
            off = lax.rem(b - z - step + 2 * ZS, ZS) // 4
            wbuf[at : at + count] = filt[f, a, off, k, cc, d, u : u + count]

    y_at = 1 - by

    def first_conv(n):
        a, b = divmod(n, 3)
        load_chunk(0, n)

        def one(i, carry):
            lhs = field[pl.ds(NX * i + a, NX), pl.ds(y_at + b, 5)].reshape(NX * 120, 768)
            part = jnp.dot(lhs, wbuf[...].reshape(768, 256), preferred_element_type=F32)
            rows = pl.ds(NX * i, NX)
            part = part.reshape(NX, 5, 24, 256)
            acc[rows] = part if n == 0 else acc[rows] + part
            return carry

        lax.fori_loop(0, 10 // NX, one, 0)

    def activate_hidden():
        def activate(i, carry):
            ok = (i + 8 * bx >= 1) & (i + 8 * bx < 65)
            low = bz == 0
            hid[i, 5 * by] = jnp.zeros((16, 768), BF16)
            for j in range(5):
                h = jnp.where(ok, gelu(acc[i, j]), 0.0)
                none = jnp.zeros((1, 256), F32)
                edge = h[16:17]
                hid[i, y_at + j, :, 0:256] = jnp.concatenate(
                    [jnp.where(low, none, edge), h[0:15]], axis=0
                ).astype(BF16)
                hid[i, y_at + j, :, 256:512] = h[0:16].astype(BF16)
                hid[i, y_at + j, :, 512:768] = jnp.concatenate(
                    [h[1:16], jnp.where(low, edge, none)], axis=0
                ).astype(BF16)
            return carry

        lax.fori_loop(0, 10, activate, 0)


    def run(what, f=0, off=0):
        if what == "near":
            wait_near(off)
            start(0, off, 0)
            start(1, off, 0)
        elif what == "far":
            arrived(blk(off, 0), far + {3: 0, 1: 1, 2: 2}[off])
            if off != 1:
                send_near(off)
                return
            for n, pos in enumerate((xp, xm, xo)):
                send(side_block(x), side_block(x), side + n, device(pos, y, z, c))
        elif what == "side":
            for n, pos in enumerate((xm, xp, xo)):
                arrived(side_block(pos), side + n)
            start(0, 1, 0)
            start(1, 1, 0)
        elif what == "turn0":
            turn(f, off, 0)
        elif what == "end0":
            end(f, off, 0)
            start(f, off, 1)
        elif what == "turn1":
            turn(f, off, 1)
        elif what == "end1":
            end(f, off, 1)
        elif what == "conv":
            first_conv(f)
        elif what == "sib":
            from_sib(f)
        elif what == "edges":
            edges()
        elif what == "sums":
            send_sums()
        elif what == "shift":
            shift_field()
        else:
            for d in range(1, 8):
                arrived(gall.at[c, lax.rem(q + 8 - d, 8)], gs + d - 1)
            send(gall.at[c], gall.at[c], gs + 7, sib_dev)

    send_near(0)
    for act in PLAN:
        run(*act)
    activate_hidden()

    from_sib(1)
    for n in range(9):
        a, b = divmod(n, 3)
        load_chunk(1, n)
        lhs = hid[a : a + 8, b : b + 4].reshape(512, 768)
        part = jnp.dot(lhs, wbuf[...].reshape(768, 256), preferred_element_type=F32)
        part = part.reshape(8, 4, 16, 256)
        conv[...] = part if n == 0 else conv[...] + part

    arrived(gall.at[1 - c], gs + 7)
    sums[...] = gall[...]
    for f in range(2):
        for g in range(4):
            n = min(7, UNITS - 7 * g)
            pan[f, 7 * g : 7 * g + n] = filt[f, yhi, 0, 0, g // 2, g % 2, 0:n]
    for copy in sent:
        copy.wait_send()


def outputs(owned, conv, gall, mom1, mom2, feat, mom1_out, mom2_out, held, sem):
    copy = pltpu.make_async_copy(conv, held, sem)
    copy.start()
    for f in range(2):
        here = owned[f] == 1
        for d in range(16):
            dc, dl, dx = d // 8, d // 4 % 2, d % 4
            for u in range(2):
                at = 7 * (2 * dc + dl) + 2 * dx + u
                if 2 * dx + u > 6 or at >= UNITS:
                    continue
                g = gall[dc, d % 8, f, u].astype(F32)
                m, v = mom1[f, at], mom2[f, at]
                mom1_out[f, at] = jnp.where(here, 0.9 * m + 0.1 * g, m)
                mom2_out[f, at] = jnp.where(here, 0.95 * v + 0.05 * (g * g), v)
    copy.wait()

    def finish(i, carry):
        feat[i] = gelu(held[i]).astype(BF16)
        return carry

    lax.fori_loop(0, 8, finish, 0)


def shards(volumes, grad_parts, master, mom1, mom2, owner):
    def units(a):
        return a.reshape(2, UNITS, 8, 256)

    vmem = pl.BlockSpec(memory_space=pltpu.VMEM)
    n_sems = 16 + N_A2A + N_HALO + N_RING + 16 + N_SIB + 8 + N_G
    state = jax.ShapeDtypeStruct((2, UNITS, 8, 256), F32)
    smem = pl.BlockSpec(memory_space=pltpu.SMEM)
    args = (units(mom1[0]), units(mom2[0]))
    conv, pan, gall = pl.pallas_call(
        body,
        out_shape=(
            jax.ShapeDtypeStruct((8, 4, 16, 256), F32),
            jax.ShapeDtypeStruct((2, UNITS, 8, 256), BF16),
            jax.ShapeDtypeStruct((2, 8, 2, 2, 8, 256), BF16),
        ),
        in_specs=[smem] + [vmem] * 5,
        out_specs=[vmem] * 3,
        scratch_shapes=[
            pltpu.VMEM((2, 8, 2, 3, 2, 8, 256), BF16),
            pltpu.VMEM((8, 2, 3, 2, 8, 256), BF16),
            pltpu.VMEM((8, 2, 3, 2, 8, 256), BF16),
            pltpu.VMEM((2, 2, 8, 256), BF16),
            pltpu.VMEM((2, 8, 2, 2, 8, 256), BF16),
            pltpu.VMEM((2, 2, 4, 4, 2, 2, 8, 8, 256), BF16),
            pltpu.VMEM((12, 8, 16, 256), BF16),
            pltpu.VMEM((12, 16, 256), BF16),
            pltpu.VMEM((12, 16, 256), BF16),
            pltpu.VMEM((12, 8, 24, 768), BF16),
            pltpu.VMEM((10, 5, 24, 256), F32),
            pltpu.VMEM((10, 6, 16, 768), BF16),
            pltpu.VMEM((96, 8, 256), BF16),
            pltpu.SemaphoreType.DMA((n_sems,)),
            pltpu.SemaphoreType.DMA((n_sems,)),
        ],
        compiler_params=pltpu.CompilerParams(
            collective_id=0, has_side_effects=True, vmem_limit_bytes=56 << 20
        ),
    )(owner, volumes[0, 0], units(grad_parts[0]), units(master), *args)
    s, r = lax.axis_index("space"), lax.axis_index("rep")
    owned = (lax.dynamic_slice_in_dim(owner, s, 1, 1)[:, 0] == r).astype(jnp.int32)
    feat, m_out, v_out = pl.pallas_call(
        outputs,
        out_shape=(jax.ShapeDtypeStruct((8, 4, 16, 256), BF16), state, state),
        in_specs=[smem, pl.BlockSpec(memory_space=pl.ANY)] + [vmem] * 3,
        out_specs=[vmem] * 3,
        scratch_shapes=[pltpu.VMEM((8, 4, 16, 256), F32), pltpu.SemaphoreType.DMA],
        compiler_params=pltpu.CompilerParams(vmem_limit_bytes=16 << 20),
    )(owned, conv, gall, *args)
    rows = lax.dynamic_slice_in_dim(pan.reshape(2, 216, 256), 27 * (r // 2), 27, 1)
    rows = rows.astype(F32).reshape(2, 2, 3456)
    share = lax.dynamic_index_in_dim(rows, lax.rem(r, 2), 1, keepdims=False)
    return (
        feat[None, None],
        share,
        m_out.reshape(1, 2, 216, 256),
        v_out.reshape(1, 2, 216, 256),
    )


def solution(mesh):
    placed = (
        P("rep", "space", None, None, None, None),
        P("rep", None, "space", None),
        P(None, "space", None),
        P("rep", None, "space", None),
        P("rep", None, "space", None),
        P(),
    )
    return jax.shard_map(
        shards,
        mesh=mesh,
        in_specs=placed,
        out_specs=(
            P("rep", "space", None, None, None, None),
            P(None, ("space", "rep")),
            P("rep", None, "space", None),
            P("rep", None, "space", None),
        ),
        check_vma=False,
    )
```

```python
import jax
import jax.numpy as jnp
from jax import lax
from jax.experimental import pallas as pl
from jax.experimental.pallas import tpu as pltpu
from jax.sharding import PartitionSpec as P

MESH = pl.DeviceIdType.MESH
F32 = jnp.float32
BF16 = jnp.bfloat16
UNITS = 27
ZS = 16
NX = 5
N_A2A, N_HALO, N_RING, N_SIB, N_G = 7, 6, 48, 24, 8

PLAN = (
    ("near", 0, 0), ("far", 0, 1), ("far", 0, 3), ("turn0", 0, 0), ("turn0", 1, 0), ("side", 0, 1), ("end0", 0, 0),
    ("far", 0, 2), ("near", 0, 3), ("turn0", 0, 1), ("turn0", 1, 1), ("turn0", 1, 3), ("near", 0, 2), ("edges",),
    ("end0", 1, 0), ("turn1", 0, 0), ("turn0", 0, 3), ("turn0", 1, 2), ("turn0", 0, 2), ("end1", 0, 0),
    ("end0", 0, 3), ("end0", 0, 1), ("end0", 1, 3), ("end0", 0, 2), ("turn1", 1, 0), ("end0", 1, 1), ("turn1", 0, 3),
    ("turn1", 0, 1), ("shift",), ("end0", 1, 2), ("sums",), ("turn1", 0, 2), ("end1", 0, 1), ("end1", 0, 3),
    ("turn1", 1, 3), ("turn1", 1, 1), ("end1", 0, 2), ("end1", 1, 0), ("turn1", 1, 2), ("sib", 0), ("conv", 0),
    ("conv", 1), ("end1", 1, 3), ("end1", 1, 1), ("end1", 1, 2), ("conv", 2), ("conv", 3), ("conv", 4), ("gs",),
    ("conv", 5), ("conv", 6), ("conv", 7), ("conv", 8),
)


def unit_of(row_unit):
    panel, within = divmod(row_unit, UNITS)
    group, place = divmod(within, 7)
    return panel // ZS, panel % ZS, group // 2, group % 2, place


def runs_of(chunk):
    runs = []
    for k in range(96):
        at = unit_of(96 * chunk + k)
        if runs and runs[-1][1][:4] == at[:4] and runs[-1][1][4] + runs[-1][2] == at[4]:
            runs[-1][2] += 1
        else:
            runs.append([k, at, 1])
    return runs


def gelu(v):
    return 0.5 * v * (1.0 + jnp.tanh(0.7978845608028654 * (v + 0.044715 * (v * v * v))))


def body(
    owner, vol, grads, master, mom1, mom2,
    conv, pan, sums,
    stage, paired, got, gsum, gall, filt, raw, edge_out, edge_in, field, acc, hid, wbuf,
    bar_send, bar_recv,
):
    s = lax.axis_index("space")
    r = lax.axis_index("rep")
    yhi, z = s // ZS, lax.rem(s, ZS)
    ylo, x, c = r // 8, lax.rem(r // 2, 4), lax.rem(r, 2)
    y = 2 * yhi + ylo
    bx, by, bz = s // 4, lax.rem(s // 2, 2), lax.rem(s, 2)

    def device(px, py, pz, pc):
        return (py // 2 * ZS + pz, lax.rem(py, 2) * 8 + 2 * px + pc)

    q = 4 * ylo + x
    xp, xm, xo = lax.rem(x + 1, 4), lax.rem(x + 3, 4), lax.rem(x + 2, 4)
    yp, ym, yo = lax.rem(y + 1, 4), lax.rem(y + 3, 4), lax.rem(y + 2, 4)
    zh, zl = z // 4, lax.rem(z, 4)
    lp, lm, lo = lax.rem(zl + 1, 4), lax.rem(zl + 3, 4), lax.rem(zl + 2, 4)

    def along_z(n):
        return device(x, y, lax.rem(z + n + ZS, ZS), c)

    sib_dev = device(x, y, z, 1 - c)
    other_y = jnp.where(ylo == 0, ym, yp)

    def chip(n):
        return (s, 2 * n + c)

    flip = 2 - 4 * by
    halo_peers = []
    for dx, fl in ((-1, 0), (1, 0), (0, 1), (-1, 1), (1, 1)):
        halo_peers.append((dx, fl, (lax.rem(s + fl * flip + 4 * dx + 32, 32), r)))

    barrier = pltpu.get_barrier_semaphore()
    all_peers = [sib_dev] + [chip(lax.rem(q + d, 8)) for d in range(1, 8)]
    all_peers += [along_z(n) for n in (4, -4, 8, 1, -1, 2, -2)] + [device(x, other_y, z, c)]
    all_peers += [p for _, _, p in halo_peers]
    for p in all_peers:
        pl.semaphore_signal(barrier, inc=1, device_id=p, device_id_type=MESH)

    for d in range(16):
        dc, dl, dx = d // 8, d // 4 % 2, d % 4
        first = 7 * (2 * dc + dl) + 2 * dx
        for u in range(2):
            at = min(first + (u if dx < 3 else 0), UNITS - 1)
            stage[dc, d % 8, :, 0, u] = grads[:, at]
            stage[dc, d % 8, :, 1, u] = mom1[:, at].astype(BF16)
            stage[dc, d % 8, :, 2, u] = mom2[:, at].astype(BF16)

    pl.semaphore_wait(barrier, len(all_peers))

    sent = []
    base = [0]

    def take(n):
        base[0] += n
        return base[0] - n

    def send(src, dst, k, dev):
        copy = pltpu.make_async_remote_copy(
            src_ref=src, dst_ref=dst, send_sem=bar_send.at[k], recv_sem=bar_recv.at[k],
            device_id=dev, device_id_type=MESH,
        )
        copy.start()
        sent.append(copy)

    def arrived(dst, k):
        pltpu.make_async_remote_copy(
            src_ref=dst, dst_ref=dst, send_sem=bar_send.at[k], recv_sem=bar_recv.at[k],
            device_id=(s, r), device_id_type=MESH,
        ).wait_recv()

    pair = take(1)
    send(stage.at[1 - c], paired, pair, sib_dev)
    halo = take(N_HALO)
    x_src = {-1: (0, 2), 0: (0, 8), 1: (6, 2)}
    x_dst = {-1: 10, 0: 2, 1: 0}
    for k, (dx, fl, dev) in enumerate(halo_peers):
        sx, nx = x_src[dx]
        sy, dy, ny = (2 * (1 - by), 6 * by, 2) if fl else (0, 2, 4)
        send(
            vol.at[pl.ds(sx, nx), pl.ds(sy, ny)],
            raw.at[pl.ds(x_dst[dx], nx), pl.ds(dy, ny)],
            halo + k, dev,
        )

    arrived(paired, pair)
    a2a = take(N_A2A)
    sib_owns = [owner[f, s] == 2 * q + 1 - c for f in range(2)]
    for d in range(1, 9):
        to = lax.rem(q + d, 8)
        for f in range(2):
            g = stage[c, to, f, 0].astype(F32) + paired[to, f, 0].astype(F32)
            stage[c, to, f, 0] = g.astype(BF16)
            for k in (1, 2):
                mine, other = stage[c, to, f, k], paired[to, f, k]
                stage[c, to, f, k] = jnp.where(sib_owns[f], other.astype(F32), mine.astype(F32)).astype(BF16)
        if d < 8:
            send(stage.at[c, to], got.at[q], a2a + d - 1, chip(to))
    got[q] = stage[c, q]
    raw[2:10, 2:6] = vol[...]

    for d in range(1, 8):
        arrived(got.at[lax.rem(q + 8 - d, 8)], a2a + d - 1)
    first = 7 * (2 * c + ylo) + 2 * x
    corr_one = 1.0 - 0.9**10
    corr_two = 1.0 - 0.95**10
    for f in range(2):
        own = owner[f, s] // 2
        for u in range(2):
            total = got[0, f, 0, u].astype(F32)
            for k in range(1, 8):
                total = total + got[k, f, 0, u].astype(F32)
            m_new = 0.9 * got[own, f, 1, u].astype(F32) + 0.1 * total
            v_new = 0.95 * got[own, f, 2, u].astype(F32) + 0.05 * (total * total)
            w = master[f, jnp.minimum(first + u, UNITS - 1)]
            step = m_new / corr_one / (jnp.sqrt(v_new / corr_two) + 1e-08) + 0.1 * w
            gsum[f, u] = total.astype(BF16)
            filt[f, yhi, 0, 0, c, ylo, 2 * x + u] = (w - 0.004 * step).astype(BF16)

    mine = pl.ds(2 * x, 2)

    def blk(off, k):
        return filt.at[:, yhi, off, k, c, ylo, mine]

    far = take(3)
    send(blk(0, 0), blk(3, 0), far, along_z(4))
    send(blk(0, 0), blk(1, 0), far + 1, along_z(-4))
    send(blk(0, 0), blk(2, 0), far + 2, along_z(8))
    near = {off: take(3) for off in (0, 3, 2)}

    def send_near(off):
        send(blk(off, 0), blk(off, 3), near[off], along_z(1))
        send(blk(off, 0), blk(off, 1), near[off] + 1, along_z(-1))
        send(blk(off, 0), blk(off, 2), near[off] + 2, along_z(2 - 4 * yhi))

    def wait_near(off):
        for n, k in enumerate((3, 1, 2)):
            arrived(blk(off, k), near[off] + n)

    side = take(3)

    def side_block(pos):
        return filt.at[:, yhi, 1, 0, c, ylo, pl.ds(2 * pos, 2)]

    kinds = {
        (0, 0): 1, (1, 0): 0, (0, 3): 0, (1, 3): 1, (0, 2): 1, (1, 2): 0, (0, 1): 2, (1, 1): 2,
    }
    ring = take(N_RING + 16)
    sib = take(N_SIB + 8)
    ways = {
        "x": (x, xp, xm, xo, device(xp, y, z, c), device(xm, y, z, c)),
        "y": (y, yp, ym, yo, device(x, yp, z, c), device(x, ym, z, c)),
        "z": (0, 1, 3, 2, along_z(1), along_z(-1)),
    }
    order = {0: "yx", 1: "xy", 2: "yz"}

    def ring_of(f, off, phase):
        n = ring + 4 * (8 * f + 2 * off + phase)
        kind = kinds[f, off]

        def reg(pos, half=None, core=c):
            if kind == 2:
                if phase == 0:
                    u0, nu = {None: (0, 7), 0: (0, 4), 1: (4, 3)}[half]
                    return filt.at[f, pos // 2, off, 0, core, lax.rem(pos, 2), pl.ds(u0, nu)]
                hi = pl.ds(0, 2) if half is None else pl.ds(half, 1)
                return filt.at[f, hi, off, pos, core, :, pl.ds(0, 7)]
            ks = pl.ds(0, 4) if half is None else pl.ds(2 * half, 2)
            if kind == 0 and phase == 0:
                return filt.at[f, pos // 2, off, ks, core, lax.rem(pos, 2), mine]
            if kind == 0:
                hi = pl.ds(0, 2) if half is None else pl.ds(half, 1)
                return filt.at[f, hi, off, :, core, :, pl.ds(2 * pos, 2)]
            if phase == 0:
                return filt.at[f, yhi, off, ks, core, ylo, pl.ds(2 * pos, 2)]
            return filt.at[f, pos // 2, off, ks, core, lax.rem(pos, 2), pl.ds(0, 7)]

        return (n, order[kind][phase] == "z") + ways[order[kind][phase]] + (reg,)

    def start(f, off, phase):
        n, rel, me, plus, minus, opp, to_plus, to_minus, reg = ring_of(f, off, phase)
        send(reg(me), reg(minus if rel else me), n, to_plus)
        send(reg(me), reg(plus if rel else me), n + 1, to_minus)
        if phase == 1:
            send(reg(me), reg(me), sib + 4 * (4 * f + off), sib_dev)

    def turn(f, off, phase):
        n, rel, me, plus, minus, opp, to_plus, to_minus, reg = ring_of(f, off, phase)
        arrived(reg(minus), n)
        send(reg(minus, 0), reg(opp if rel else minus, 0), n + 2, to_plus)
        arrived(reg(plus), n + 1)
        send(reg(plus, 1), reg(opp if rel else plus, 1), n + 3, to_minus)
        if phase == 1:
            m = sib + 4 * (4 * f + off)
            send(reg(minus), reg(minus), m + 1, sib_dev)
            send(reg(plus), reg(plus), m + 2, sib_dev)

    def end(f, off, phase):
        n, rel, me, plus, minus, opp, to_plus, to_minus, reg = ring_of(f, off, phase)
        arrived(reg(opp, 0), n + 2)
        arrived(reg(opp, 1), n + 3)
        if phase == 1:
            send(reg(opp), reg(opp), sib + 4 * (4 * f + off) + 3, sib_dev)

    def from_sib(f):
        for off in range(4):
            n, rel, me, plus, minus, opp, to_plus, to_minus, reg = ring_of(f, off, 1)
            for m, pos in enumerate((me, minus, plus, opp)):
                arrived(reg(pos, None, 1 - c), sib + 4 * (4 * f + off) + m)

    gs = take(N_G)

    def edges():
        for k, (dx, fl, dev) in enumerate(halo_peers):
            sx, nx = x_src[dx]
            dy, ny = (6 * (1 - by), 2) if fl else (2, 4)
            dst_x = {-1: 0, 0: 2, 1: 10}[dx]
            pairs = raw.at[pl.ds(dst_x, nx), pl.ds(dy, ny)]
            arrived(pairs, halo + {0: 1, 1: 0, 2: 2, 3: 4, 4: 3}[k])

        def pack(i, carry):
            rows = [raw[i, j].astype(F32) for j in range(8)]
            near = jnp.concatenate([jnp.where(bz == 0, v[15:16], v[0:1]) for v in rows], axis=0)
            far = jnp.concatenate([jnp.where(bz == 0, v[14:15], v[1:2]) for v in rows], axis=0)
            edge_out[i] = jnp.concatenate([near, far], axis=0).astype(BF16)
            return carry

        lax.fori_loop(0, 12, pack, 0)
        z_partner = z + 1 - 2 * bz
        send(edge_out, edge_in, halo + 5, device(x, y, z_partner, c))

    def send_sums():
        for d in range(1, 8):
            to = lax.rem(q + d, 8)
            send(gsum, gall.at[c, q], gs + d - 1, chip(to))
        gall[c, q] = gsum[...]

    def shift_field():
        arrived(edge_in, halo + 5)

        def shifts(i, carry):
            edges = edge_in[i].astype(F32)
            x_ok = (i + 8 * bx >= 2) & (i + 8 * bx < 66)
            for j in range(8):
                y_ok = (j + 4 * by >= 2) & (j + 4 * by < 10)
                ok = x_ok & y_ok
                v = jnp.where(ok, raw[i, j].astype(F32), 0.0)
                e0 = jnp.where(ok, edges[j : j + 1], 0.0)
                e1 = jnp.where(ok, edges[8 + j : 9 + j], 0.0)
                none = jnp.zeros((1, 256), F32)
                rest = jnp.zeros((7, 256), F32)
                low = bz == 0
                field[i, j, :, 0:256] = jnp.concatenate(
                    [jnp.where(low, none, e0), v[0:15], jnp.where(low, v[15:16], e1), rest], axis=0
                ).astype(BF16)
                field[i, j, :, 256:512] = jnp.concatenate([v, e0, rest], axis=0).astype(BF16)
                field[i, j, :, 512:768] = jnp.concatenate(
                    [v[1:16], jnp.where(low, e0, none), jnp.where(low, e1, v[0:1]), rest], axis=0
                ).astype(BF16)
            return carry

        lax.fori_loop(0, 12, shifts, 0)

    def load_chunk(f, n):
        for at, (a, b, cc, d, u), count in runs_of(n):
            k = lax.rem(b - z + ZS, 4)
            step = k - 4 * (k // (2 + a))
            off = lax.rem(b - z - step + 2 * ZS, ZS) // 4
            wbuf[at : at + count] = filt[f, a, off, k, cc, d, u : u + count]

    y_at = 1 - by

    def first_conv(n):
        a, b = divmod(n, 3)
        load_chunk(0, n)

        def one(i, carry):
            lhs = field[pl.ds(NX * i + a, NX), pl.ds(y_at + b, 5)].reshape(NX * 120, 768)
            part = jnp.dot(lhs, wbuf[...].reshape(768, 256), preferred_element_type=F32)
            rows = pl.ds(NX * i, NX)
            part = part.reshape(NX, 5, 24, 256)
            acc[rows] = part if n == 0 else acc[rows] + part
            return carry

        lax.fori_loop(0, 10 // NX, one, 0)

    def activate_hidden():
        def activate(i, carry):
            ok = (i + 8 * bx >= 1) & (i + 8 * bx < 65)
            low = bz == 0
            hid[i, 5 * by] = jnp.zeros((16, 768), BF16)
            for j in range(5):
                h = jnp.where(ok, gelu(acc[i, j]), 0.0)
                none = jnp.zeros((1, 256), F32)
                edge = h[16:17]
                hid[i, y_at + j, :, 0:256] = jnp.concatenate(
                    [jnp.where(low, none, edge), h[0:15]], axis=0
                ).astype(BF16)
                hid[i, y_at + j, :, 256:512] = h[0:16].astype(BF16)
                hid[i, y_at + j, :, 512:768] = jnp.concatenate(
                    [h[1:16], jnp.where(low, edge, none)], axis=0
                ).astype(BF16)
            return carry

        lax.fori_loop(0, 10, activate, 0)


    def run(what, f=0, off=0):
        if what == "near":
            wait_near(off)
            start(0, off, 0)
            start(1, off, 0)
        elif what == "far":
            arrived(blk(off, 0), far + {3: 0, 1: 1, 2: 2}[off])
            if off != 1:
                send_near(off)
                return
            for n, pos in enumerate((xp, xm, xo)):
                send(side_block(x), side_block(x), side + n, device(pos, y, z, c))
        elif what == "side":
            for n, pos in enumerate((xm, xp, xo)):
                arrived(side_block(pos), side + n)
            start(0, 1, 0)
            start(1, 1, 0)
        elif what == "turn0":
            turn(f, off, 0)
        elif what == "end0":
            end(f, off, 0)
            start(f, off, 1)
        elif what == "turn1":
            turn(f, off, 1)
        elif what == "end1":
            end(f, off, 1)
        elif what == "conv":
            first_conv(f)
        elif what == "sib":
            from_sib(f)
        elif what == "edges":
            edges()
        elif what == "sums":
            send_sums()
        elif what == "shift":
            shift_field()
        else:
            for d in range(1, 8):
                arrived(gall.at[c, lax.rem(q + 8 - d, 8)], gs + d - 1)
            send(gall.at[c], gall.at[c], gs + 7, sib_dev)

    send_near(0)
    for act in PLAN:
        run(*act)
    activate_hidden()

    from_sib(1)
    for n in range(9):
        a, b = divmod(n, 3)
        load_chunk(1, n)
        lhs = hid[a : a + 8, b : b + 4].reshape(512, 768)
        part = jnp.dot(lhs, wbuf[...].reshape(768, 256), preferred_element_type=F32)
        part = part.reshape(8, 4, 16, 256)
        conv[...] = part if n == 0 else conv[...] + part

    arrived(gall.at[1 - c], gs + 7)
    sums[...] = gall[...]
    for f in range(2):
        for g in range(4):
            n = min(7, UNITS - 7 * g)
            pan[f, 7 * g : 7 * g + n] = filt[f, yhi, 0, 0, g // 2, g % 2, 0:n]
    for copy in sent:
        copy.wait_send()


def outputs(owner, conv, gall, mom1, mom2, pan, feat, mom1_out, mom2_out, rows, held, panel, sem):
    s = lax.axis_index("space")
    r = lax.axis_index("rep")
    copy = pltpu.make_async_copy(conv, held, sem)
    copy.start()
    for f in range(2):
        here = owner[f, s] == r
        for d in range(16):
            dc, dl, dx = d // 8, d // 4 % 2, d % 4
            for u in range(2):
                at = 7 * (2 * dc + dl) + 2 * dx + u
                if 2 * dx + u > 6 or at >= UNITS:
                    continue
                g = gall[dc, d % 8, f, u].astype(F32)
                m, v = mom1[f, at], mom2[f, at]
                mom1_out[f, at] = jnp.where(here, 0.9 * m + 0.1 * g, m)
                mom2_out[f, at] = jnp.where(here, 0.95 * v + 0.05 * (g * g), v)
    for f in range(2):
        panel[f, 0:UNITS] = pan[f].astype(F32)
        panel[f, UNITS] = jnp.zeros((8, 256), F32)
        at = 27 * (r // 2)
        near = panel[f, pl.ds(at // 8, 5)].reshape(40, 256)
        rows[f] = pltpu.roll(near, lax.rem(40 - lax.rem(at, 8), 40), 0)[0:27]
    copy.wait()

    def finish(i, carry):
        feat[i] = gelu(held[i]).astype(BF16)
        return carry

    lax.fori_loop(0, 8, finish, 0)


def shards(volumes, grad_parts, master, mom1, mom2, owner):
    def units(a):
        return a.reshape(2, UNITS, 8, 256)

    vmem = pl.BlockSpec(memory_space=pltpu.VMEM)
    n_sems = 16 + N_A2A + N_HALO + N_RING + 16 + N_SIB + 8 + N_G
    state = jax.ShapeDtypeStruct((2, UNITS, 8, 256), F32)
    smem = pl.BlockSpec(memory_space=pltpu.SMEM)
    args = (units(mom1[0]), units(mom2[0]))
    conv, pan, gall = pl.pallas_call(
        body,
        out_shape=(
            jax.ShapeDtypeStruct((8, 4, 16, 256), F32),
            jax.ShapeDtypeStruct((2, UNITS, 8, 256), BF16),
            jax.ShapeDtypeStruct((2, 8, 2, 2, 8, 256), BF16),
        ),
        in_specs=[smem] + [vmem] * 5,
        out_specs=[vmem] * 3,
        scratch_shapes=[
            pltpu.VMEM((2, 8, 2, 3, 2, 8, 256), BF16),
            pltpu.VMEM((8, 2, 3, 2, 8, 256), BF16),
            pltpu.VMEM((8, 2, 3, 2, 8, 256), BF16),
            pltpu.VMEM((2, 2, 8, 256), BF16),
            pltpu.VMEM((2, 8, 2, 2, 8, 256), BF16),
            pltpu.VMEM((2, 2, 4, 4, 2, 2, 8, 8, 256), BF16),
            pltpu.VMEM((12, 8, 16, 256), BF16),
            pltpu.VMEM((12, 16, 256), BF16),
            pltpu.VMEM((12, 16, 256), BF16),
            pltpu.VMEM((12, 8, 24, 768), BF16),
            pltpu.VMEM((10, 5, 24, 256), F32),
            pltpu.VMEM((10, 6, 16, 768), BF16),
            pltpu.VMEM((96, 8, 256), BF16),
            pltpu.SemaphoreType.DMA((n_sems,)),
            pltpu.SemaphoreType.DMA((n_sems,)),
        ],
        compiler_params=pltpu.CompilerParams(
            collective_id=0, has_side_effects=True, vmem_limit_bytes=56 << 20
        ),
    )(owner, volumes[0, 0], units(grad_parts[0]), units(master), *args)
    feat, m_out, v_out, rows = pl.pallas_call(
        outputs,
        out_shape=(
            jax.ShapeDtypeStruct((8, 4, 16, 256), BF16),
            state,
            state,
            jax.ShapeDtypeStruct((2, 27, 256), F32),
        ),
        in_specs=[smem, pl.BlockSpec(memory_space=pl.ANY)] + [vmem] * 4,
        out_specs=[vmem] * 4,
        scratch_shapes=[
            pltpu.VMEM((8, 4, 16, 256), F32),
            pltpu.VMEM((2, UNITS + 1, 8, 256), F32),
            pltpu.SemaphoreType.DMA,
        ],
        compiler_params=pltpu.CompilerParams(vmem_limit_bytes=56 << 20),
    )(owner, conv, gall, *args, pan)
    share = lax.dynamic_index_in_dim(
        rows.reshape(2, 2, 3456), lax.rem(lax.axis_index("rep"), 2), 1, keepdims=False
    )
    return (
        feat[None, None],
        share,
        m_out.reshape(1, 2, 216, 256),
        v_out.reshape(1, 2, 216, 256),
    )


def solution(mesh):
    placed = (
        P("rep", "space", None, None, None, None),
        P("rep", None, "space", None),
        P(None, "space", None),
        P("rep", None, "space", None),
        P("rep", None, "space", None),
        P(),
    )
    return jax.shard_map(
        shards,
        mesh=mesh,
        in_specs=placed,
        out_specs=(
            P("rep", "space", None, None, None, None),
            P(None, ("space", "rep")),
            P("rep", None, "space", None),
            P("rep", None, "space", None),
        ),
        check_vma=False,
    )
```

```python
import jax
import jax.numpy as jnp
from jax import lax
from jax.experimental import pallas as pl
from jax.experimental.pallas import tpu as pltpu
from jax.sharding import PartitionSpec as P

MESH = pl.DeviceIdType.MESH
F32 = jnp.float32
BF16 = jnp.bfloat16
UNITS = 27
ZS = 16
NX = 5
N_A2A, N_HALO, N_RING, N_SIB, N_G = 7, 6, 48, 24, 8

PLAN = (
    ("near", 0, 0), ("far", 0, 1), ("far", 0, 3), ("turn0", 0, 0), ("turn0", 1, 0), ("side", 0, 1), ("end0", 0, 0),
    ("far", 0, 2), ("near", 0, 3), ("turn0", 0, 1), ("turn0", 1, 1), ("turn0", 1, 3), ("near", 0, 2), ("edges",),
    ("end0", 1, 0), ("turn1", 0, 0), ("turn0", 0, 3), ("turn0", 1, 2), ("turn0", 0, 2), ("end1", 0, 0),
    ("end0", 0, 3), ("end0", 0, 1), ("end0", 1, 3), ("end0", 0, 2), ("turn1", 1, 0), ("end0", 1, 1), ("turn1", 0, 3),
    ("turn1", 0, 1), ("shift",), ("end0", 1, 2), ("sums",), ("turn1", 0, 2), ("end1", 0, 1), ("end1", 0, 3),
    ("turn1", 1, 3), ("turn1", 1, 1), ("end1", 0, 2), ("end1", 1, 0), ("turn1", 1, 2), ("sib", 0), ("conv", 0),
    ("conv", 1), ("end1", 1, 3), ("end1", 1, 1), ("end1", 1, 2), ("conv", 2), ("conv", 3), ("conv", 4), ("gs",),
    ("conv", 5), ("conv", 6), ("conv", 7), ("conv", 8),
)


def unit_of(row_unit):
    panel, within = divmod(row_unit, UNITS)
    group, place = divmod(within, 7)
    return panel // ZS, panel % ZS, group // 2, group % 2, place


def runs_of(chunk):
    runs = []
    for k in range(96):
        at = unit_of(96 * chunk + k)
        if runs and runs[-1][1][:4] == at[:4] and runs[-1][1][4] + runs[-1][2] == at[4]:
            runs[-1][2] += 1
        else:
            runs.append([k, at, 1])
    return runs


def gelu(v):
    return 0.5 * v * (1.0 + jnp.tanh(0.7978845608028654 * (v + 0.044715 * (v * v * v))))


def body(
    owner, vol, grads, master, mom1, mom2,
    conv, pan, sums,
    stage, paired, got, gsum, gall, filt, raw, edge_out, edge_in, field, acc, hid, wbuf,
    bar_send, bar_recv,
):
    s = lax.axis_index("space")
    r = lax.axis_index("rep")
    yhi, z = s // ZS, lax.rem(s, ZS)
    ylo, x, c = r // 8, lax.rem(r // 2, 4), lax.rem(r, 2)
    y = 2 * yhi + ylo
    bx, by, bz = s // 4, lax.rem(s // 2, 2), lax.rem(s, 2)

    def device(px, py, pz, pc):
        return (py // 2 * ZS + pz, lax.rem(py, 2) * 8 + 2 * px + pc)

    q = 4 * ylo + x
    xp, xm, xo = lax.rem(x + 1, 4), lax.rem(x + 3, 4), lax.rem(x + 2, 4)
    yp, ym, yo = lax.rem(y + 1, 4), lax.rem(y + 3, 4), lax.rem(y + 2, 4)
    zh, zl = z // 4, lax.rem(z, 4)
    lp, lm, lo = lax.rem(zl + 1, 4), lax.rem(zl + 3, 4), lax.rem(zl + 2, 4)

    def along_z(n):
        return device(x, y, lax.rem(z + n + ZS, ZS), c)

    sib_dev = device(x, y, z, 1 - c)
    other_y = jnp.where(ylo == 0, ym, yp)

    def chip(n):
        return (s, 2 * n + c)

    flip = 2 - 4 * by
    halo_peers = []
    for dx, fl in ((-1, 0), (1, 0), (0, 1), (-1, 1), (1, 1)):
        halo_peers.append((dx, fl, (lax.rem(s + fl * flip + 4 * dx + 32, 32), r)))

    barrier = pltpu.get_barrier_semaphore()
    all_peers = [sib_dev] + [chip(lax.rem(q + d, 8)) for d in range(1, 8)]
    all_peers += [along_z(n) for n in (4, -4, 8, 1, -1, 2, -2)] + [device(x, other_y, z, c)]
    all_peers += [p for _, _, p in halo_peers]
    for p in all_peers:
        pl.semaphore_signal(barrier, inc=1, device_id=p, device_id_type=MESH)

    for d in range(16):
        dc, dl, dx = d // 8, d // 4 % 2, d % 4
        first = 7 * (2 * dc + dl) + 2 * dx
        for u in range(2):
            at = min(first + (u if dx < 3 else 0), UNITS - 1)
            stage[dc, d % 8, :, 0, u] = grads[:, at]
            stage[dc, d % 8, :, 1, u] = mom1[:, at].astype(BF16)
            stage[dc, d % 8, :, 2, u] = mom2[:, at].astype(BF16)

    pl.semaphore_wait(barrier, len(all_peers))

    sent = []
    base = [0]

    def take(n):
        base[0] += n
        return base[0] - n

    def send(src, dst, k, dev):
        copy = pltpu.make_async_remote_copy(
            src_ref=src, dst_ref=dst, send_sem=bar_send.at[k], recv_sem=bar_recv.at[k],
            device_id=dev, device_id_type=MESH,
        )
        copy.start()
        sent.append(copy)

    def arrived(dst, k):
        pltpu.make_async_remote_copy(
            src_ref=dst, dst_ref=dst, send_sem=bar_send.at[k], recv_sem=bar_recv.at[k],
            device_id=(s, r), device_id_type=MESH,
        ).wait_recv()

    pair = take(1)
    send(stage.at[1 - c], paired, pair, sib_dev)
    halo = take(N_HALO)
    inside = {-1: bx > 0, 0: bx >= 0, 1: bx < 7}
    halo_sent = []
    x_src = {-1: (0, 2), 0: (0, 8), 1: (6, 2)}
    x_dst = {-1: 10, 0: 2, 1: 0}
    for k, (dx, fl, dev) in enumerate(halo_peers):
        sx, nx = x_src[dx]
        sy, dy, ny = (2 * (1 - by), 6 * by, 2) if fl else (0, 2, 4)
        copy = pltpu.make_async_remote_copy(
            src_ref=vol.at[pl.ds(sx, nx), pl.ds(sy, ny)],
            dst_ref=raw.at[pl.ds(x_dst[dx], nx), pl.ds(dy, ny)],
            send_sem=bar_send.at[halo + k], recv_sem=bar_recv.at[halo + k],
            device_id=dev, device_id_type=MESH,
        )
        pl.when(inside[dx])(copy.start)
        halo_sent.append((inside[dx], copy))

    arrived(paired, pair)
    a2a = take(N_A2A)
    sib_owns = [owner[f, s] == 2 * q + 1 - c for f in range(2)]
    for d in range(1, 9):
        to = lax.rem(q + d, 8)
        for f in range(2):
            g = stage[c, to, f, 0].astype(F32) + paired[to, f, 0].astype(F32)
            stage[c, to, f, 0] = g.astype(BF16)
            for k in (1, 2):
                mine, other = stage[c, to, f, k], paired[to, f, k]
                stage[c, to, f, k] = jnp.where(sib_owns[f], other.astype(F32), mine.astype(F32)).astype(BF16)
        if d < 8:
            send(stage.at[c, to], got.at[q], a2a + d - 1, chip(to))
    got[q] = stage[c, q]
    raw[2:10, 2:6] = vol[...]

    for d in range(1, 8):
        arrived(got.at[lax.rem(q + 8 - d, 8)], a2a + d - 1)
    first = 7 * (2 * c + ylo) + 2 * x
    corr_one = 1.0 - 0.9**10
    corr_two = 1.0 - 0.95**10
    for f in range(2):
        own = owner[f, s] // 2
        for u in range(2):
            total = got[0, f, 0, u].astype(F32)
            for k in range(1, 8):
                total = total + got[k, f, 0, u].astype(F32)
            m_new = 0.9 * got[own, f, 1, u].astype(F32) + 0.1 * total
            v_new = 0.95 * got[own, f, 2, u].astype(F32) + 0.05 * (total * total)
            w = master[f, jnp.minimum(first + u, UNITS - 1)]
            step = m_new / corr_one / (jnp.sqrt(v_new / corr_two) + 1e-08) + 0.1 * w
            gsum[f, u] = total.astype(BF16)
            filt[f, yhi, 0, 0, c, ylo, 2 * x + u] = (w - 0.004 * step).astype(BF16)

    mine = pl.ds(2 * x, 2)

    def blk(off, k):
        return filt.at[:, yhi, off, k, c, ylo, mine]

    far = take(3)
    send(blk(0, 0), blk(3, 0), far, along_z(4))
    send(blk(0, 0), blk(1, 0), far + 1, along_z(-4))
    send(blk(0, 0), blk(2, 0), far + 2, along_z(8))
    near = {off: take(3) for off in (0, 3, 2)}

    def send_near(off):
        send(blk(off, 0), blk(off, 3), near[off], along_z(1))
        send(blk(off, 0), blk(off, 1), near[off] + 1, along_z(-1))
        send(blk(off, 0), blk(off, 2), near[off] + 2, along_z(2 - 4 * yhi))

    def wait_near(off):
        for n, k in enumerate((3, 1, 2)):
            arrived(blk(off, k), near[off] + n)

    side = take(3)

    def side_block(pos):
        return filt.at[:, yhi, 1, 0, c, ylo, pl.ds(2 * pos, 2)]

    kinds = {
        (0, 0): 1, (1, 0): 0, (0, 3): 0, (1, 3): 1, (0, 2): 1, (1, 2): 0, (0, 1): 2, (1, 1): 2,
    }
    ring = take(N_RING + 16)
    sib = take(N_SIB + 8)
    ways = {
        "x": (x, xp, xm, xo, device(xp, y, z, c), device(xm, y, z, c)),
        "y": (y, yp, ym, yo, device(x, yp, z, c), device(x, ym, z, c)),
        "z": (0, 1, 3, 2, along_z(1), along_z(-1)),
    }
    order = {0: "yx", 1: "xy", 2: "yz"}

    def ring_of(f, off, phase):
        n = ring + 4 * (8 * f + 2 * off + phase)
        kind = kinds[f, off]

        def reg(pos, half=None, core=c):
            if kind == 2:
                if phase == 0:
                    u0, nu = {None: (0, 7), 0: (0, 4), 1: (4, 3)}[half]
                    return filt.at[f, pos // 2, off, 0, core, lax.rem(pos, 2), pl.ds(u0, nu)]
                hi = pl.ds(0, 2) if half is None else pl.ds(half, 1)
                return filt.at[f, hi, off, pos, core, :, pl.ds(0, 7)]
            ks = pl.ds(0, 4) if half is None else pl.ds(2 * half, 2)
            if kind == 0 and phase == 0:
                return filt.at[f, pos // 2, off, ks, core, lax.rem(pos, 2), mine]
            if kind == 0:
                hi = pl.ds(0, 2) if half is None else pl.ds(half, 1)
                return filt.at[f, hi, off, :, core, :, pl.ds(2 * pos, 2)]
            if phase == 0:
                return filt.at[f, yhi, off, ks, core, ylo, pl.ds(2 * pos, 2)]
            return filt.at[f, pos // 2, off, ks, core, lax.rem(pos, 2), pl.ds(0, 7)]

        return (n, order[kind][phase] == "z") + ways[order[kind][phase]] + (reg,)

    def start(f, off, phase):
        n, rel, me, plus, minus, opp, to_plus, to_minus, reg = ring_of(f, off, phase)
        send(reg(me), reg(minus if rel else me), n, to_plus)
        send(reg(me), reg(plus if rel else me), n + 1, to_minus)
        if phase == 1:
            send(reg(me), reg(me), sib + 4 * (4 * f + off), sib_dev)

    def turn(f, off, phase):
        n, rel, me, plus, minus, opp, to_plus, to_minus, reg = ring_of(f, off, phase)
        arrived(reg(minus), n)
        send(reg(minus, 0), reg(opp if rel else minus, 0), n + 2, to_plus)
        arrived(reg(plus), n + 1)
        send(reg(plus, 1), reg(opp if rel else plus, 1), n + 3, to_minus)
        if phase == 1:
            m = sib + 4 * (4 * f + off)
            send(reg(minus), reg(minus), m + 1, sib_dev)
            send(reg(plus), reg(plus), m + 2, sib_dev)

    def end(f, off, phase):
        n, rel, me, plus, minus, opp, to_plus, to_minus, reg = ring_of(f, off, phase)
        arrived(reg(opp, 0), n + 2)
        arrived(reg(opp, 1), n + 3)
        if phase == 1:
            send(reg(opp), reg(opp), sib + 4 * (4 * f + off) + 3, sib_dev)

    def from_sib(f):
        for off in range(4):
            n, rel, me, plus, minus, opp, to_plus, to_minus, reg = ring_of(f, off, 1)
            for m, pos in enumerate((me, minus, plus, opp)):
                arrived(reg(pos, None, 1 - c), sib + 4 * (4 * f + off) + m)

    gs = take(N_G)

    def edges():
        for k, (dx, fl, dev) in enumerate(halo_peers):
            sx, nx = x_src[dx]
            dy, ny = (6 * (1 - by), 2) if fl else (2, 4)
            dst_x = {-1: 0, 0: 2, 1: 10}[dx]
            pairs = raw.at[pl.ds(dst_x, nx), pl.ds(dy, ny)]
            n = halo + {0: 1, 1: 0, 2: 2, 3: 4, 4: 3}[k]

            @pl.when(inside[dx])
            def _(pairs=pairs, n=n):
                arrived(pairs, n)


        def pack(i, carry):
            rows = [raw[i, j].astype(F32) for j in range(8)]
            near = jnp.concatenate([jnp.where(bz == 0, v[15:16], v[0:1]) for v in rows], axis=0)
            far = jnp.concatenate([jnp.where(bz == 0, v[14:15], v[1:2]) for v in rows], axis=0)
            edge_out[i] = jnp.concatenate([near, far], axis=0).astype(BF16)
            return carry

        lax.fori_loop(0, 12, pack, 0)
        z_partner = z + 1 - 2 * bz
        send(edge_out, edge_in, halo + 5, device(x, y, z_partner, c))

    def send_sums():
        for d in range(1, 8):
            to = lax.rem(q + d, 8)
            send(gsum, gall.at[c, q], gs + d - 1, chip(to))
        gall[c, q] = gsum[...]

    def shift_field():
        arrived(edge_in, halo + 5)

        def shifts(i, carry):
            edges = edge_in[i].astype(F32)
            x_ok = (i + 8 * bx >= 2) & (i + 8 * bx < 66)
            for j in range(8):
                y_ok = (j + 4 * by >= 2) & (j + 4 * by < 10)
                ok = x_ok & y_ok
                v = jnp.where(ok, raw[i, j].astype(F32), 0.0)
                e0 = jnp.where(ok, edges[j : j + 1], 0.0)
                e1 = jnp.where(ok, edges[8 + j : 9 + j], 0.0)
                none = jnp.zeros((1, 256), F32)
                rest = jnp.zeros((7, 256), F32)
                low = bz == 0
                field[i, j, :, 0:256] = jnp.concatenate(
                    [jnp.where(low, none, e0), v[0:15], jnp.where(low, v[15:16], e1), rest], axis=0
                ).astype(BF16)
                field[i, j, :, 256:512] = jnp.concatenate([v, e0, rest], axis=0).astype(BF16)
                field[i, j, :, 512:768] = jnp.concatenate(
                    [v[1:16], jnp.where(low, e0, none), jnp.where(low, e1, v[0:1]), rest], axis=0
                ).astype(BF16)
            return carry

        lax.fori_loop(0, 12, shifts, 0)

    def load_chunk(f, n):
        for at, (a, b, cc, d, u), count in runs_of(n):
            k = lax.rem(b - z + ZS, 4)
            step = k - 4 * (k // (2 + a))
            off = lax.rem(b - z - step + 2 * ZS, ZS) // 4
            wbuf[at : at + count] = filt[f, a, off, k, cc, d, u : u + count]

    y_at = 1 - by

    def first_conv(n):
        a, b = divmod(n, 3)
        load_chunk(0, n)

        def one(i, carry):
            lhs = field[pl.ds(NX * i + a, NX), pl.ds(y_at + b, 5)].reshape(NX * 120, 768)
            part = jnp.dot(lhs, wbuf[...].reshape(768, 256), preferred_element_type=F32)
            rows = pl.ds(NX * i, NX)
            part = part.reshape(NX, 5, 24, 256)
            acc[rows] = part if n == 0 else acc[rows] + part
            return carry

        lax.fori_loop(0, 10 // NX, one, 0)

    def activate_hidden():
        def activate(i, carry):
            ok = (i + 8 * bx >= 1) & (i + 8 * bx < 65)
            low = bz == 0
            hid[i, 5 * by] = jnp.zeros((16, 768), BF16)
            for j in range(5):
                h = jnp.where(ok, gelu(acc[i, j]), 0.0)
                none = jnp.zeros((1, 256), F32)
                edge = h[16:17]
                hid[i, y_at + j, :, 0:256] = jnp.concatenate(
                    [jnp.where(low, none, edge), h[0:15]], axis=0
                ).astype(BF16)
                hid[i, y_at + j, :, 256:512] = h[0:16].astype(BF16)
                hid[i, y_at + j, :, 512:768] = jnp.concatenate(
                    [h[1:16], jnp.where(low, edge, none)], axis=0
                ).astype(BF16)
            return carry

        lax.fori_loop(0, 10, activate, 0)


    def run(what, f=0, off=0):
        if what == "near":
            wait_near(off)
            start(0, off, 0)
            start(1, off, 0)
        elif what == "far":
            arrived(blk(off, 0), far + {3: 0, 1: 1, 2: 2}[off])
            if off != 1:
                send_near(off)
                return
            for n, pos in enumerate((xp, xm, xo)):
                send(side_block(x), side_block(x), side + n, device(pos, y, z, c))
        elif what == "side":
            for n, pos in enumerate((xm, xp, xo)):
                arrived(side_block(pos), side + n)
            start(0, 1, 0)
            start(1, 1, 0)
        elif what == "turn0":
            turn(f, off, 0)
        elif what == "end0":
            end(f, off, 0)
            start(f, off, 1)
        elif what == "turn1":
            turn(f, off, 1)
        elif what == "end1":
            end(f, off, 1)
        elif what == "conv":
            first_conv(f)
        elif what == "sib":
            from_sib(f)
        elif what == "edges":
            edges()
        elif what == "sums":
            send_sums()
        elif what == "shift":
            shift_field()
        else:
            for d in range(1, 8):
                arrived(gall.at[c, lax.rem(q + 8 - d, 8)], gs + d - 1)
            send(gall.at[c], gall.at[c], gs + 7, sib_dev)

    send_near(0)
    for act in PLAN:
        run(*act)
    activate_hidden()

    from_sib(1)
    for n in range(9):
        a, b = divmod(n, 3)
        load_chunk(1, n)
        lhs = hid[a : a + 8, b : b + 4].reshape(512, 768)
        part = jnp.dot(lhs, wbuf[...].reshape(768, 256), preferred_element_type=F32)
        rows = acc.at[0:8, 0:4, 0:16]
        part = part.reshape(8, 4, 16, 256)
        rows[...] = part if n == 0 else rows[...] + part

    def finish(i, carry):
        conv[i] = gelu(acc[i, 0:4, 0:16]).astype(BF16)
        return carry

    lax.fori_loop(0, 8, finish, 0)

    arrived(gall.at[1 - c], gs + 7)
    sums[...] = gall[...]
    for f in range(2):
        for g in range(4):
            n = min(7, UNITS - 7 * g)
            pan[f, 7 * g : 7 * g + n] = filt[f, yhi, 0, 0, g // 2, g % 2, 0:n]
    for copy in sent:
        copy.wait_send()
    for there, copy in halo_sent:
        pl.when(there)(copy.wait_send)


def outputs(owner, conv, gall, mom1, mom2, pan, feat, mom1_out, mom2_out, rows, panel, sem):
    s = lax.axis_index("space")
    r = lax.axis_index("rep")
    copy = pltpu.make_async_copy(conv, feat, sem)
    copy.start()
    for f in range(2):
        here = owner[f, s] == r
        for d in range(16):
            dc, dl, dx = d // 8, d // 4 % 2, d % 4
            for u in range(2):
                at = 7 * (2 * dc + dl) + 2 * dx + u
                if 2 * dx + u > 6 or at >= UNITS:
                    continue
                g = gall[dc, d % 8, f, u].astype(F32)
                m, v = mom1[f, at], mom2[f, at]
                mom1_out[f, at] = jnp.where(here, 0.9 * m + 0.1 * g, m)
                mom2_out[f, at] = jnp.where(here, 0.95 * v + 0.05 * (g * g), v)
    for f in range(2):
        panel[f, 0:UNITS] = pan[f].astype(F32)
        panel[f, UNITS] = jnp.zeros((8, 256), F32)
        at = 27 * (r // 2)
        near = panel[f, pl.ds(at // 8, 5)].reshape(40, 256)
        rows[f] = pltpu.roll(near, lax.rem(40 - lax.rem(at, 8), 40), 0)[0:27]
    copy.wait()


def shards(volumes, grad_parts, master, mom1, mom2, owner):
    def units(a):
        return a.reshape(2, UNITS, 8, 256)

    vmem = pl.BlockSpec(memory_space=pltpu.VMEM)
    n_sems = 16 + N_A2A + N_HALO + N_RING + 16 + N_SIB + 8 + N_G
    state = jax.ShapeDtypeStruct((2, UNITS, 8, 256), F32)
    smem = pl.BlockSpec(memory_space=pltpu.SMEM)
    args = (units(mom1[0]), units(mom2[0]))
    conv, pan, gall = pl.pallas_call(
        body,
        out_shape=(
            jax.ShapeDtypeStruct((8, 4, 16, 256), BF16),
            jax.ShapeDtypeStruct((2, UNITS, 8, 256), BF16),
            jax.ShapeDtypeStruct((2, 8, 2, 2, 8, 256), BF16),
        ),
        in_specs=[smem] + [vmem] * 5,
        out_specs=[vmem] * 3,
        scratch_shapes=[
            pltpu.VMEM((2, 8, 2, 3, 2, 8, 256), BF16),
            pltpu.VMEM((8, 2, 3, 2, 8, 256), BF16),
            pltpu.VMEM((8, 2, 3, 2, 8, 256), BF16),
            pltpu.VMEM((2, 2, 8, 256), BF16),
            pltpu.VMEM((2, 8, 2, 2, 8, 256), BF16),
            pltpu.VMEM((2, 2, 4, 4, 2, 2, 8, 8, 256), BF16),
            pltpu.VMEM((12, 8, 16, 256), BF16),
            pltpu.VMEM((12, 16, 256), BF16),
            pltpu.VMEM((12, 16, 256), BF16),
            pltpu.VMEM((12, 8, 24, 768), BF16),
            pltpu.VMEM((10, 5, 24, 256), F32),
            pltpu.VMEM((10, 6, 16, 768), BF16),
            pltpu.VMEM((96, 8, 256), BF16),
            pltpu.SemaphoreType.DMA((n_sems,)),
            pltpu.SemaphoreType.DMA((n_sems,)),
        ],
        compiler_params=pltpu.CompilerParams(
            collective_id=0, has_side_effects=True, vmem_limit_bytes=56 << 20
        ),
    )(owner, volumes[0, 0], units(grad_parts[0]), units(master), *args)
    feat, m_out, v_out, rows = pl.pallas_call(
        outputs,
        out_shape=(
            jax.ShapeDtypeStruct((8, 4, 16, 256), BF16),
            state,
            state,
            jax.ShapeDtypeStruct((2, 27, 256), F32),
        ),
        in_specs=[smem, pl.BlockSpec(memory_space=pl.ANY)] + [vmem] * 4,
        out_specs=[pl.BlockSpec(memory_space=pl.ANY)] + [vmem] * 3,
        scratch_shapes=[
            pltpu.VMEM((2, UNITS + 1, 8, 256), F32),
            pltpu.SemaphoreType.DMA,
        ],
        compiler_params=pltpu.CompilerParams(vmem_limit_bytes=62 << 20),
    )(owner, conv, gall, *args, pan)
    share = lax.dynamic_index_in_dim(
        rows.reshape(2, 2, 3456), lax.rem(lax.axis_index("rep"), 2), 1, keepdims=False
    )
    return (
        feat[None, None],
        share,
        m_out.reshape(1, 2, 216, 256),
        v_out.reshape(1, 2, 216, 256),
    )


def solution(mesh):
    placed = (
        P("rep", "space", None, None, None, None),
        P("rep", None, "space", None),
        P(None, "space", None),
        P("rep", None, "space", None),
        P("rep", None, "space", None),
        P(),
    )
    return jax.shard_map(
        shards,
        mesh=mesh,
        in_specs=placed,
        out_specs=(
            P("rep", "space", None, None, None, None),
            P(None, ("space", "rep")),
            P("rep", None, "space", None),
            P("rep", None, "space", None),
        ),
        check_vma=False,
    )
```
